256 devices in a mesh: grp: 4 (over z_hi, core), dev: 64 (over y, z_lo, x).
Axes of the slice: x: 4, y: 4, z: 8 (z_hi: 2, z_lo: 4; z = z_hi * 4 + z_lo), core: 2. Of those that a mesh axis runs over, the one named last changes fastest.
Arguments:
- images: bfloat16 [512, 16, 16, 768], P(('grp', 'dev')), may hold values from -6 to 6
- cotangent: bfloat16 [512, 16, 16, 768], P(('grp', 'dev')), may hold values from -6 to 6
- dw_kernel: float32 [7, 7, 768], replicated, may hold values from -0.875 to 0.875
- w_expand: bfloat16 [3072, 768], P('dev'), may hold values from -0.21875 to 0.21875
- w_contract: bfloat16 [3072, 768], P('dev'), may hold values from -0.109375 to 0.109375
Outputs:
- block_out: bfloat16 [512, 16, 16, 768], P(('grp', 'dev'))
- grad_images: bfloat16 [512, 16, 16, 768], P(('grp', 'dev'))
- grad_kernel: float32 [7, 7, 768], replicated
- grad_expand: float32 [3072, 768], P('dev')
- grad_contract: float32 [3072, 768], P('dev')
The draws below stay inside these ranges and needn't reach their ends.
All inputs are finite; a program needn't handle non-finite values.
Results may differ from the reference program's by a relative error of at most 0.0055.
Values may be sent and summed in bfloat16 or wider, within the bound.
A program may use at most 128 MiB of HBM per device.

```python
import math
import jax
import jax.numpy as jnp
from jax import lax

C = 768
FF = 3072
KS = 7
SIDE = 16
IMAGES = 512


def levels(key, dims, cuts, least, largest):
    level, own = 1.0, jax.random.fold_in(key, 6)
    for position, parts in cuts:
        draws = jnp.exp(jax.random.uniform(jax.random.fold_in(own, position), (parts,), jnp.float32, least / len(cuts), largest / len(cuts)))
        level = level * jnp.repeat(draws, dims[position] // parts).reshape([-1 if axis == position else 1 for axis in range(len(dims))])
    return level


def scatter_about(rng, shape, spread, bound, cuts=(), kind=jnp.bfloat16):
    values = jax.random.normal(rng, shape, jnp.float32) * spread
    if len(cuts) > 0:
        values = levels(rng, shape, cuts, -0.22, 0.18) * values
    return jnp.clip(values, min=-bound, max=bound).astype(kind)


def setup_inputs(seed: int = 0) -> dict:
    key_list = jax.random.split(jax.random.key(seed), 6)
    images = scatter_about(key_list[0], (IMAGES, SIDE, SIDE, C), 1.0, 6.0, ((0, 256),))
    cotangent = scatter_about(key_list[1], (IMAGES, SIDE, SIDE, C), 1.0, 6.0, ((0, 256),))
    dw_kernel = scatter_about(key_list[2], (KS, KS, C), (KS * KS) ** -0.5, 0.875, (), jnp.float32)
    w_expand = scatter_about(key_list[3], (FF, C), C ** -0.5, 0.21875, ((0, 64),))
    w_contract = scatter_about(key_list[4], (FF, C), FF ** -0.5, 0.109375, ((0, 64),))
    return {"images": images, "cotangent": cotangent, "dw_kernel": dw_kernel, "w_expand": w_expand, "w_contract": w_contract}


SQRT_HALF = 0.7071067811865476
INV_ROOT_TWO_PI = 0.3989422804014327
EPSILON = 1e-06

def depthwise(values, kernel):
    side_len = values.shape[1]
    reach = kernel.shape[0] // 2
    padded = jnp.pad(values, ((0, 0), (reach, reach), (reach, reach), (0, 0)))
    result = jnp.zeros(values.shape, jnp.float32)
    for row_off in range(kernel.shape[0]):
        for col_off in range(kernel.shape[1]):
            result = result + padded[:, row_off:row_off + side_len, col_off:col_off + side_len, :] * kernel[row_off, col_off]
    return result

def conv_back(upstream, kernel):
    side_len = upstream.shape[1]
    reach = kernel.shape[0] // 2
    width = kernel.shape[0] - 1
    padded = jnp.pad(upstream, ((0, 0), (reach, reach), (reach, reach), (0, 0)))
    result = jnp.zeros(upstream.shape, jnp.float32)
    for row_off in range(kernel.shape[0]):
        for col_off in range(kernel.shape[1]):
            result = result + padded[:, width - row_off:width - row_off + side_len, width - col_off:width - col_off + side_len, :] * kernel[row_off, col_off]
    return result

def kernel_term(upstream, values, kernel):
    side_len = values.shape[1]
    reach = kernel.shape[0] // 2
    padded = jnp.pad(values, ((0, 0), (reach, reach), (reach, reach), (0, 0)))
    pieces = []
    for row_off in range(kernel.shape[0]):
        for col_off in range(kernel.shape[1]):
            pieces.append(lax.optimization_barrier(jnp.sum(upstream * padded[:, row_off:row_off + side_len, col_off:col_off + side_len, :], axis=(0, 1, 2))))
    return jnp.stack(pieces).reshape(kernel.shape)

def block_step(images, cotangent, dw_kernel, w_expand, w_contract):
    channels = images.shape[3]
    tok_rows = images.shape[0] * images.shape[1] * images.shape[2]
    as_float = images.astype(jnp.float32)
    conv_out = depthwise(as_float, dw_kernel).reshape(tok_rows, channels)
    average = lax.optimization_barrier(jnp.mean(conv_out, axis=1, keepdims=True))
    centred = conv_out - average
    variance = lax.optimization_barrier(jnp.mean(centred * centred, axis=1, keepdims=True))
    inv_std = lax.rsqrt(variance + EPSILON)
    standard = centred * inv_std
    normed = standard.astype(jnp.bfloat16)
    pre_act = jnp.dot(normed, w_expand.T, preferred_element_type=jnp.float32)
    normal_cdf = 0.5 * (1.0 + jax.scipy.special.erf(pre_act * SQRT_HALF))
    activated = (pre_act * normal_cdf).astype(jnp.bfloat16)
    mixed = jnp.dot(activated, w_contract, preferred_element_type=jnp.float32)
    block_out = (as_float.reshape(tok_rows, channels) + mixed).astype(jnp.bfloat16).reshape(images.shape)
    upstream = cotangent.reshape(tok_rows, channels)
    act_grad = jnp.dot(upstream, w_contract.T, preferred_element_type=jnp.float32)
    slope = normal_cdf + pre_act * jnp.exp(-0.5 * pre_act * pre_act) * INV_ROOT_TWO_PI
    pre_grad = (act_grad * slope).astype(jnp.bfloat16)
    norm_grad = jnp.dot(pre_grad, w_expand, preferred_element_type=jnp.float32)
    conv_grad = inv_std * (norm_grad - lax.optimization_barrier(jnp.mean(norm_grad, axis=1, keepdims=True)) - standard * lax.optimization_barrier(jnp.mean(norm_grad * standard, axis=1, keepdims=True)))
    conv_grad = conv_grad.reshape(images.shape)
    grad_images = (cotangent.astype(jnp.float32) + conv_back(conv_grad, dw_kernel)).astype(jnp.bfloat16)
    kernel_part = kernel_term(conv_grad, as_float, dw_kernel)
    expand_part = jnp.dot(pre_grad.T, normed, preferred_element_type=jnp.float32)
    contract_part = jnp.dot(activated.T, upstream, preferred_element_type=jnp.float32)
    return (block_out, grad_images, kernel_part, expand_part, contract_part)

def reference(images, cotangent, dw_kernel, w_expand, w_contract):
    number = images.shape[0]
    block_len = math.gcd(number, 32)
    blocks = number // block_len
    image_blocks = images.reshape((blocks, block_len) + images.shape[1:])
    cot_blocks = cotangent.reshape((blocks, block_len) + cotangent.shape[1:])

    def step_fn(running, inputs):
        block_out, grad_images, kernel_part, expand_part, contract_part = block_step(inputs[0], inputs[1], dw_kernel, w_expand, w_contract)
        running = (running[0] + kernel_part, running[1] + expand_part, running[2] + contract_part)
        return (running, (block_out, grad_images))
    start_sums = (jnp.zeros(dw_kernel.shape, jnp.float32), jnp.zeros(w_expand.shape, jnp.float32), jnp.zeros(w_contract.shape, jnp.float32))
    sums, outputs = lax.scan(step_fn, start_sums, (image_blocks, cot_blocks))
    grad_scale = float(images.shape[0] * images.shape[1] * images.shape[2]) ** (-0.5)
    block_out = outputs[0].reshape(images.shape)
    grad_images = outputs[1].reshape(images.shape)
    return (block_out, grad_images, sums[0] * grad_scale, sums[1] * grad_scale, sums[2] * grad_scale)
```

```python
import functools

import jax
import jax.numpy as jnp
from jax import lax
from jax.experimental import pallas as pl
from jax.experimental.pallas import tpu as pltpu
from jax.sharding import PartitionSpec as P

MESH = pl.DeviceIdType.MESH
F32, BF16 = jnp.float32, jnp.bfloat16
SQRT_HALF = 0.7071067811865476
INV_ROOT_TWO_PI = 0.3989422804014327
EPSILON = 1e-06
NT = (((1,), (1,)), ((), ()))
NN = (((1,), (0,)), ((), ()))
TN = (((0,), (0,)), ((), ()))

C = 768
TOK = 512
ROWS = 16
ORDERS = (("x", "y", "z"), ("y", "z", "x"), ("z", "x", "y"))
SIZE = {"x": 2, "y": 4, "z": 4}


def dot(a, b, dims):
    return lax.dot_general(a, b, dims, preferred_element_type=F32)


def sizes(part):
    n = [SIZE[a] for a in ORDERS[part]]
    return (1, n[0], n[0] * n[1])


class Place:
    def __init__(self):
        grp, dev = lax.axis_index("grp"), lax.axis_index("dev")
        self.hi, self.core = grp // 2, grp % 2
        self.y, self.zlo, self.x = dev // 16, (dev // 4) % 4, dev % 4
        self.z = self.hi * 4 + self.zlo
        self.source = (self.x % 2) == self.core
        self.other = (self.x % 2) != self.core

    def device(self, x, y, z, core):
        return {"grp": (z // 4) * 2 + core, "dev": (y * 4 + z % 4) * 4 + x}

    def peer(self, axis, off, core=None):
        core = self.core if core is None else core
        x, y, z = self.x, self.y, self.z
        if axis == "x":
            x = (x + off + 4) % 4
        elif axis == "y":
            y = (y + off + 4) % 4
        else:
            z = (z + off + 8) % 8
        return self.device(x, y, z, core)

    def slot(self, axis, off=0):
        if axis == "x":
            return ((self.x + off + 4) % 4) // 2
        if axis == "y":
            return (self.y + off + 4) % 4
        return (self.zlo + off + 4) % 4

    def block(self, part, phase):
        order = ORDERS[part]
        n = [SIZE[a] for a in order]
        i = [self.slot(a) for a in order]
        if phase == 0:
            return (i[2] * n[1] + i[1]) * n[0] + i[0], 1
        if phase == 1:
            return (i[2] * n[1] + i[1]) * n[0], n[0]
        return i[2] * n[1] * n[0], n[0] * n[1]


def moves(axis):
    if axis == "z":
        return ((1, None, 0), (-1, None, 1), (2, 0, 2), (-2, 1, 3))
    return ((1, None, 0), (-1, None, 1), (2, None, 2))


def when(cond, fn):
    if cond is None:
        fn()
    else:
        pl.when(cond)(fn)


def kernel(
    img_ref, cot_ref, dwk_ref, we_ref, wc_ref,
    out_ref, gimg_ref, gker_ref, ge_ref, gc_ref,
    buf, grads, nrm2, cot2, mix, ngr, ex_send, ex_recv, conv, inv, pad, kacc,
    kall, kr0, ksum, krx, ky, kz, fin, finf,
    rb0, rb1, rb2, rb3, rb4, rb5, rb6, rb7, rb8,
    t0, t1, t2, t3, t4, t5, t6, t7, t8,
    bsem_s, bsem_r, rsem_s, rsem_r, esem_s, esem_r, ksem_s, ksem_r, fsem_s, fsem_r,
):
    rbufs = ((rb0, rb1, rb2), (rb3, rb4, rb5), (rb6, rb7, rb8))
    tbufs = ((t0, t1, t2), (t3, t4, t5), (t6, t7, t8))
    at = Place()
    partner = at.device(at.x, at.y, at.z, 1 - at.core)

    barrier = pltpu.get_barrier_semaphore()
    friends = [at.peer("x", o) for o in (1, -1, 2)] + [at.peer("y", o) for o in (1, -1, 2)]
    friends += [at.peer("z", o) for o in range(1, 8)] + [partner]
    friends += [at.peer("x", o, 1 - at.core) for o in (1, -1, 2)]
    for friend in friends:
        pl.semaphore_signal(barrier, inc=1, device_id=friend, device_id_type=MESH)
    pl.semaphore_wait(barrier, len(friends))

    def copy(src, dst, send, recv, to):
        return pltpu.make_async_remote_copy(
            src_ref=src, dst_ref=dst, send_sem=send, recv_sem=recv,
            device_id=to, device_id_type=MESH,
        )

    def gather_copies(part, phase):
        axis = ORDERS[part][phase]
        px = ORDERS[part].index("x")
        start, count = at.block(part, phase)
        out = []
        for off, half, j in moves(axis):
            if half is None:
                ref = buf.at[part, :, pl.ds(start, count)]
            else:
                ref = buf.at[part, half, pl.ds(start, count)]
            cp = copy(ref, ref, bsem_s.at[part, phase, j], bsem_r.at[part, phase, j], at.peer(axis, off))
            if phase < px:
                send_if = recv_if = at.source
            elif phase == px:
                send_if = at.source
                recv_if = at.source if j == 2 else at.other
            else:
                send_if = recv_if = None
            out.append((cp, send_if, recv_if))
        return out

    def gather_start(phase, parts=(0, 1, 2)):
        for part in parts:
            for cp, send_if, _ in gather_copies(part, phase):
                when(send_if, cp.start)

    def gather_wait(phase, parts=(0, 1, 2)):
        for part in parts:
            for cp, send_if, recv_if in gather_copies(part, phase):
                when(send_if, cp.wait_send)
                when(recv_if, cp.wait_recv)

    @pl.when(at.source)
    def _():
        for part in range(3):
            start, _n = at.block(part, 0)
            buf[part, 0, start] = we_ref[part * ROWS : (part + 1) * ROWS]
            buf[part, 1, start] = wc_ref[part * ROWS : (part + 1) * ROWS]

    gather_start(0)
    cot_copy = copy(cot_ref, cot2.at[1], esem_s.at[0], esem_r.at[0], partner)
    cot_copy.start()

    pad[...] = jnp.zeros_like(pad)

    def windows(values):
        pad[3:19, 8:24, :] = values.reshape(16, 16, 128)

    def conv_step(i, source, target, flip, finish):
        image, block = i // 6, i % 6
        lanes = pl.ds(pl.multiple_of(block * 128, 128), 128)
        windows(source[pl.ds(pl.multiple_of(image * 256, 256), 256), lanes].astype(F32))
        for half in range(2):
            acc = jnp.zeros((8, 16, 128), F32)
            for q in range(7):
                shifted = pad[half * 8 : half * 8 + 14, 5 + q : 21 + q, :]
                for p in range(7):
                    tap = 48 - (p * 7 + q) if flip else p * 7 + q
                    acc = acc + shifted[p : p + 8] * dwk_ref[tap : tap + 1, lanes].reshape(1, 1, 128)
            rows = pl.ds(pl.multiple_of(image * 256 + half * 128, 128), 128)
            target[rows, lanes] = finish(acc.reshape(128, 128), rows, lanes)

    def forward(i, carry):
        conv_step(i, img_ref, conv, False, lambda v, rows, lanes: v)

        @pl.when(i == 6)
        def _():
            gather_wait(0)
            gather_start(1)

        return carry

    lax.fori_loop(0, 12, forward, 0)

    def norm(i, carry):
        rows = pl.ds(pl.multiple_of(i * 64, 64), 64)
        v = conv[rows, :]
        centred = v - jnp.mean(v, axis=1, keepdims=True)
        istd = lax.rsqrt(jnp.mean(centred * centred, axis=1, keepdims=True) + EPSILON)
        nrm2[0, rows, :] = (centred * istd).astype(BF16)
        inv[rows, :] = jnp.broadcast_to(istd, (64, 128))
        cot2[0, rows, :] = cot_ref[rows, :]
        mix[0, rows, :] = img_ref[rows, :].astype(F32)
        mix[1, rows, :] = jnp.zeros((64, C), F32)
        ngr[0, rows, :] = jnp.zeros((64, C), F32)
        ngr[1, rows, :] = jnp.zeros((64, C), F32)
        return carry

    lax.fori_loop(0, 8, norm, 0)
    nrm_copy = copy(nrm2.at[0], nrm2.at[1], esem_s.at[1], esem_r.at[1], partner)
    nrm_copy.start()
    gather_wait(1)
    gather_start(2)
    cot_copy.wait()
    nrm_copy.wait()
    gather_wait(2)

    def part_step(part, carry):
        normed = nrm2[...].reshape(2 * TOK, C)
        upstream = cot2[...].reshape(2 * TOK, C)
        expand = buf[part, 0].reshape(512, C)
        contract = buf[part, 1].reshape(512, C)
        pre_act = dot(normed, expand, NT)
        act_grad = dot(upstream, contract, NT)
        cdf = 0.5 * (1.0 + lax.erf(pre_act * SQRT_HALF))
        activated = (pre_act * cdf).astype(BF16)
        slope = cdf + pre_act * jnp.exp(-0.5 * pre_act * pre_act) * INV_ROOT_TWO_PI
        pre_grad = (act_grad * slope).astype(BF16)
        mix[...] += dot(activated, contract, NN).reshape(2, TOK, C)
        ngr[...] += dot(pre_grad, expand, NN).reshape(2, TOK, C)
        grads[part, 0] = dot(pre_grad, normed, TN).astype(BF16).reshape(32, ROWS, C)
        grads[part, 1] = dot(activated, upstream, TN).astype(BF16).reshape(32, ROWS, C)
        return carry

    lax.fori_loop(0, 3, part_step, 0)

    def reduce_copies(part, phase):
        axis = ORDERS[part][phase]
        px = ORDERS[part].index("x")
        count = sizes(part)[phase]
        src = grads.at[part] if phase == 2 else tbufs[part][phase + 1]
        out = []
        for off, half, j in moves(axis):
            pieces = pl.ds(at.slot(axis, off) * count, count)
            if half is None:
                a, b = src.at[:, pieces], rbufs[part][phase].at[j]
            else:
                a, b = src.at[half, pieces], rbufs[part][phase].at[2, half]
            cp = copy(a, b, rsem_s.at[part, phase, j], rsem_r.at[part, phase, j], at.peer(axis, off))
            if phase < px:
                send_if = recv_if = at.source
            elif phase == px:
                send_if = at.source if j == 2 else at.other
                recv_if = at.source
            else:
                send_if = recv_if = None
            out.append((cp, send_if, recv_if))
        return out

    def reduce_start(phase):
        for part in range(3):
            for cp, send_if, _ in reduce_copies(part, phase):
                when(send_if, cp.start)

    def reduce_wait(phase):
        for part in range(3):
            for cp, send_if, recv_if in reduce_copies(part, phase):
                when(send_if, cp.wait_send)
                when(recv_if, cp.wait_recv)
            axis = ORDERS[part][phase]
            count = sizes(part)[phase]
            recv, dst = rbufs[part][phase], tbufs[part][phase]
            mine = at.slot(axis) * count

            def add():
                def piece(i, carry):
                    for side in range(2):
                        if phase == 2:
                            own = grads[part, side, mine + i]
                        else:
                            own = tbufs[part][phase + 1][side, mine + i]
                        total = own.astype(F32) + recv[0, side, i].astype(F32)
                        total = total + recv[1, side, i].astype(F32) + recv[2, side, i].astype(F32)
                        dst[side, i] = total.astype(BF16)
                    return carry

                lax.fori_loop(0, count, piece, 0)

            when(at.source if phase <= ORDERS[part].index("x") else None, add)

    reduce_start(2)

    def to_send(i, carry):
        rows = pl.ds(pl.multiple_of(i * 64, 64), 64)
        ex_send[0, rows, :] = ngr[1, rows, :].astype(BF16)
        ex_send[1, rows, :] = mix[1, rows, :].astype(BF16)
        return carry

    lax.fori_loop(0, 8, to_send, 0)
    ex_copy = copy(ex_send, ex_recv, esem_s.at[2], esem_r.at[2], partner)
    ex_copy.start()
    ex_copy.wait()

    def norm_back(i, carry):
        rows = pl.ds(pl.multiple_of(i * 64, 64), 64)
        out_ref[rows, :] = (mix[0, rows, :] + ex_recv[1, rows, :].astype(F32)).astype(BF16)
        grad = ngr[0, rows, :] + ex_recv[0, rows, :].astype(F32)
        standard = nrm2[0, rows, :].astype(F32)
        mean = jnp.mean(grad, axis=1, keepdims=True)
        along = jnp.mean(grad * standard, axis=1, keepdims=True)
        conv[rows, :] = inv[rows, 0:1] * (grad - mean - standard * along)
        return carry

    lax.fori_loop(0, 8, norm_back, 0)

    def kernel_terms(block, carry):
        lanes = pl.ds(pl.multiple_of(block * 128, 128), 128)
        for image in range(2):
            windows(img_ref[image * 256 : image * 256 + 256, lanes].astype(F32))
            for half in range(2):
                first = image * 256 + half * 128
                g = conv[first : first + 128, lanes].reshape(8, 16, 128)
                for q in range(7):
                    shifted = pad[half * 8 : half * 8 + 14, 5 + q : 21 + q, :]
                    for p in range(7):
                        r = jnp.sum((g * shifted[p : p + 8]).reshape(16, 8, 128), axis=0)
                        if image == 0 and half == 0:
                            kacc[p * 7 + q, :, lanes] = r
                        else:
                            kacc[p * 7 + q, :, lanes] += r
        return carry

    lax.fori_loop(0, 6, kernel_terms, 0)
    kall[49:64, :] = jnp.zeros((15, C), F32)
    kall[0:49, :] = jnp.sum(kacc[...], axis=1)

    k0_copy = copy(kall.at[pl.ds((1 - at.core) * 32, 32)], kr0, ksem_s.at[0], ksem_r.at[0], partner)
    k0_copy.start()

    def kx_copies():
        return [
            copy(ksum.at[pl.ds(((at.x + off + 4) % 4) * 8, 8)], krx.at[j], ksem_s.at[1 + j], ksem_r.at[1 + j], at.peer("x", off))
            for j, off in enumerate((1, -1, 2))
        ]

    def ky_copies():
        return [
            copy(ky.at[at.y], ky.at[at.y], ksem_s.at[4 + j], ksem_r.at[4 + j], at.peer("y", off))
            for j, off in enumerate((1, -1, 2))
        ]

    def kz_copies():
        return [
            copy(kz.at[at.z], kz.at[at.z], ksem_s.at[7 + j], ksem_r.at[7 + j], at.peer("z", off))
            for j, off in enumerate(range(1, 8))
        ]

    share = pl.ds(at.core * 32 + at.x * 8, 8)

    def kg_copies():
        targets = [partner] + [at.peer("x", off, core) for off in (1, -1, 2) for core in (at.core, 1 - at.core)]
        return [copy(finf.at[share], finf.at[share], ksem_s.at[14 + j], ksem_r.at[14 + j], to) for j, to in enumerate(targets)]

    def start_all(copies):
        for cp in copies:
            cp.start()

    def wait_all(copies):
        for cp in copies:
            cp.wait()

    def backward(i, carry):
        conv_step(
            i, conv, gimg_ref, True,
            lambda v, rows, lanes: (v + cot_ref[rows, lanes].astype(F32)).astype(BF16),
        )

        @pl.when(i == 1)
        def _():
            k0_copy.wait()
            ksum[...] = kall[pl.ds(pl.multiple_of(at.core * 32, 32), 32), :] + kr0[...]
            start_all(kx_copies())

        @pl.when(i == 6)
        def _():
            wait_all(kx_copies())
            ky[at.y] = ksum[pl.ds(pl.multiple_of(at.x * 8, 8), 8), :] + krx[0] + krx[1] + krx[2]
            start_all(ky_copies())

        return carry

    lax.fori_loop(0, 12, backward, 0)
    wait_all(ky_copies())
    kz[at.z] = ky[0] + ky[1] + ky[2] + ky[3]
    start_all(kz_copies())

    reduce_wait(2)
    reduce_start(1)
    wait_all(kz_copies())
    total = kz[0]
    for i in range(1, 8):
        total = total + kz[i]
    finf[pl.ds(pl.multiple_of(at.core * 32 + at.x * 8, 8), 8), :] = total
    start_all(kg_copies())
    reduce_wait(1)
    reduce_start(0)
    scale = float(TOK * 256) ** (-0.5)
    wait_all(kg_copies())
    gker_ref[...] = finf[0:49, :] * scale
    reduce_wait(0)

    far = at.peer("z", 4)

    def far_copy():
        return copy(fin.at[at.hi], fin.at[at.hi], fsem_s.at[0], fsem_r.at[0], far)

    def near_copies():
        return [
            copy(ge_ref, ge_ref, fsem_s.at[1], fsem_r.at[1], partner),
            copy(gc_ref, gc_ref, fsem_s.at[2], fsem_r.at[2], partner),
        ]

    @pl.when(at.source)
    def _():
        for part in range(3):
            for side in range(2):
                fin[at.hi, side, part] = tbufs[part][0][side, 0]
        far_copy().start()
        far_copy().wait()
        for side, ref in ((0, ge_ref), (1, gc_ref)):
            for part in range(3):
                total = fin[0, side, part].astype(F32) + fin[1, side, part].astype(F32)
                ref[part * ROWS : (part + 1) * ROWS, :] = total * scale
        for cp in near_copies():
            cp.start()
        for cp in near_copies():
            cp.wait_send()

    @pl.when(at.other)
    def _():
        for cp in near_copies():
            cp.wait_recv()


def per_device(images, cotangent, dw_kernel, w_expand, w_contract):
    vmem = lambda: pl.BlockSpec(memory_space=pltpu.VMEM)
    scratch = [
        pltpu.VMEM((3, 2, 32, ROWS, C), BF16),
        pltpu.VMEM((3, 2, 32, ROWS, C), BF16),
        pltpu.VMEM((2, TOK, C), BF16),
        pltpu.VMEM((2, TOK, C), BF16),
        pltpu.VMEM((2, TOK, C), F32),
        pltpu.VMEM((2, TOK, C), F32),
        pltpu.VMEM((2, TOK, C), BF16),
        pltpu.VMEM((2, TOK, C), BF16),
        pltpu.VMEM((TOK, C), F32),
        pltpu.VMEM((TOK, 128), F32),
        pltpu.VMEM((22, 32, 128), F32),
        pltpu.VMEM((49, 8, C), F32),
        pltpu.VMEM((64, C), F32),
        pltpu.VMEM((32, C), F32),
        pltpu.VMEM((32, C), F32),
        pltpu.VMEM((3, 8, C), F32),
        pltpu.VMEM((4, 8, C), F32),
        pltpu.VMEM((8, 8, C), F32),
        pltpu.VMEM((2, 2, 3, ROWS, C), BF16),
        pltpu.VMEM((64, C), F32),
    ]
    for part in range(3):
        for phase in range(3):
            scratch.append(pltpu.VMEM((3, 2, sizes(part)[phase], ROWS, C), BF16))
    for part in range(3):
        for phase in range(3):
            scratch.append(pltpu.VMEM((2, sizes(part)[phase], ROWS, C), BF16))
    scratch += [pltpu.SemaphoreType.DMA((3, 3, 4))] * 4
    scratch += [pltpu.SemaphoreType.DMA((3,))] * 2
    scratch += [pltpu.SemaphoreType.DMA((21,))] * 2
    scratch += [pltpu.SemaphoreType.DMA((3,))] * 2
    out, gimg, gker, ge, gc = pl.pallas_call(
        kernel,
        name="block_step",
        out_shape=(
            jax.ShapeDtypeStruct((TOK, C), BF16),
            jax.ShapeDtypeStruct((TOK, C), BF16),
            jax.ShapeDtypeStruct((49, C), F32),
            jax.ShapeDtypeStruct((48, C), F32),
            jax.ShapeDtypeStruct((48, C), F32),
        ),
        in_specs=[vmem() for _ in range(5)],
        out_specs=tuple(vmem() for _ in range(5)),
        scratch_shapes=scratch,
        compiler_params=pltpu.CompilerParams(
            collective_id=0, has_side_effects=True, vmem_limit_bytes=63 * 2**20
        ),
        cost_estimate=pl.CostEstimate(flops=15 * 10**9, bytes_accessed=10**7, transcendentals=10**6),
    )(
        images.reshape(TOK, C),
        cotangent.reshape(TOK, C),
        dw_kernel.reshape(49, C),
        w_expand,
        w_contract,
    )
    return out.reshape(images.shape), gimg.reshape(images.shape), gker.reshape(7, 7, C), ge, gc


def solution(mesh):
    tokens = P(("grp", "dev"), None, None, None)
    rows = P("dev", None)
    return jax.shard_map(
        per_device,
        mesh=mesh,
        in_specs=(tokens, tokens, P(), rows, rows),
        out_specs=(tokens, tokens, P(), rows, rows),
        check_vma=False,
    )
```

```python
import functools

import jax
import jax.numpy as jnp
from jax import lax
from jax.experimental import pallas as pl
from jax.experimental.pallas import tpu as pltpu
from jax.sharding import PartitionSpec as P

MESH = pl.DeviceIdType.MESH
F32, BF16 = jnp.float32, jnp.bfloat16
SQRT_HALF = 0.7071067811865476
INV_ROOT_TWO_PI = 0.3989422804014327
EPSILON = 1e-06
NT = (((1,), (1,)), ((), ()))
NN = (((1,), (0,)), ((), ()))
TN = (((0,), (0,)), ((), ()))

C = 768
TOK = 512
ROWS = 16
SPLIT = 4
ORDERS = (("x", "y", "z"), ("y", "z", "x"), ("z", "x", "y"))
SIZE = {"x": 2, "y": 4, "z": 4}


def dot(a, b, dims):
    return lax.dot_general(a, b, dims, preferred_element_type=F32)


def sizes(part):
    n = [SIZE[a] for a in ORDERS[part]]
    return (1, n[0], n[0] * n[1])


class Place:
    def __init__(self):
        grp, dev = lax.axis_index("grp"), lax.axis_index("dev")
        self.hi, self.core = grp // 2, grp % 2
        self.y, self.zlo, self.x = dev // 16, (dev // 4) % 4, dev % 4
        self.z = self.hi * 4 + self.zlo
        self.source = (self.x % 2) == self.core
        self.other = (self.x % 2) != self.core

    def device(self, x, y, z, core):
        return {"grp": (z // 4) * 2 + core, "dev": (y * 4 + z % 4) * 4 + x}

    def peer(self, axis, off, core=None):
        core = self.core if core is None else core
        x, y, z = self.x, self.y, self.z
        if axis == "x":
            x = (x + off + 4) % 4
        elif axis == "y":
            y = (y + off + 4) % 4
        else:
            z = (z + off + 8) % 8
        return self.device(x, y, z, core)

    def slot(self, axis, off=0):
        if axis == "x":
            return ((self.x + off + 4) % 4) // 2
        if axis == "y":
            return (self.y + off + 4) % 4
        return (self.zlo + off + 4) % 4

    def share(self, part, step):
        first = (self.y, self.zlo, 2 * (self.x // 2))[part]
        return (first + step) % SPLIT

    def runs(self, part, phase):
        order = ORDERS[part]
        n = [SIZE[a] for a in order]
        i = [self.slot(a) for a in order]
        share = n[0] * n[1] // SPLIT
        if phase == 1:
            first, count = i[1] * n[0], n[0]
        else:
            first, count = i[1] * n[0] + i[0], 1
        step = min(count, share)
        return [
            (where(part, (first + k) // share, i[2]) + (first + k) % share, step)
            for k in range(0, count, step)
        ]


def where(part, s, i3):
    share = sizes(part)[2] // SPLIT
    return s * (96 // SPLIT) + part * (32 // SPLIT) + i3 * share


def moves(axis):
    if axis == "z":
        return ((1, None, 0), (-1, None, 1), (2, 0, 2), (-2, 1, 3))
    return ((1, None, 0), (-1, None, 1), (2, None, 2))


def when(cond, fn):
    if cond is None:
        fn()
    else:
        pl.when(cond)(fn)


def kernel(
    img_hbm, cot_hbm, dwk_ref, we_ref, wc_ref,
    out_hbm, gimg_hbm, gker_ref, ge_ref, gc_ref,
    img_ref, out_ref, gimg_ref, buf, grads, nrm2, cot2, mix, ngr, ex_send, ex_recv, conv, inv, pad, kacc,
    kall, krx, ky, kz, fin, finf,
    rb0, rb1, rb2, rb3, rb4, rb5, rb6, rb7, rb8,
    t0, t1, t2, t3, t4, t5, t6, t7, t8,
    bsem_s, bsem_r, rsem_s, rsem_r, esem_s, esem_r, ksem_s, ksem_r, fsem_s, fsem_r, lsem,
):
    rbufs = ((rb0, rb1, rb2), (rb3, rb4, rb5), (rb6, rb7, rb8))
    tbufs = ((t0, t1, t2), (t3, t4, t5), (t6, t7, t8))
    at = Place()
    partner = at.device(at.x, at.y, at.z, 1 - at.core)

    barrier = pltpu.get_barrier_semaphore()
    friends = [at.peer("x", o) for o in (1, -1, 2)] + [at.peer("y", o) for o in (1, -1, 2)]
    friends += [at.peer("z", o) for o in range(1, 8)] + [partner]
    friends += [at.peer("x", o, 1 - at.core) for o in (1, -1, 2)]
    for friend in friends:
        pl.semaphore_signal(barrier, inc=1, device_id=friend, device_id_type=MESH)
    img_in = pltpu.make_async_copy(img_hbm, img_ref, lsem.at[0])
    cot_in = pltpu.make_async_copy(cot_hbm, cot2.at[0], lsem.at[1])
    img_in.start()
    cot_in.start()
    pl.semaphore_wait(barrier, len(friends))

    def copy(src, dst, send, recv, to):
        return pltpu.make_async_remote_copy(
            src_ref=src, dst_ref=dst, send_sem=send, recv_sem=recv,
            device_id=to, device_id_type=MESH,
        )

    def gather_copies(part, phase, step=None):
        axis = ORDERS[part][phase]
        px = ORDERS[part].index("x")
        if phase == 2:
            share = at.share(part, step)
            runs = [(step, (where(part, share, at.slot(axis)), sizes(part)[2] // SPLIT))]
        else:
            runs = enumerate(at.runs(part, phase))
        out = []
        for r, (start, count) in runs:
            for off, half, j in moves(axis):
                if half is None:
                    ref = buf.at[:, pl.ds(start, count)]
                else:
                    ref = buf.at[half, pl.ds(start, count)]
                cp = copy(ref, ref, bsem_s.at[part, phase, r, j], bsem_r.at[part, phase, r, j], at.peer(axis, off))
                if phase < px:
                    send_if = recv_if = at.source
                elif phase == px:
                    send_if = at.source
                    recv_if = at.source if j == 2 else at.other
                else:
                    send_if = recv_if = None
                out.append((cp, send_if, recv_if))
        return out

    def gather_start(part, phase, step=None):
        for cp, send_if, _ in gather_copies(part, phase, step):
            when(send_if, cp.start)

    def gather_wait(part, phase, step=None):
        for cp, send_if, recv_if in gather_copies(part, phase, step):
            when(send_if, cp.wait_send)
            when(recv_if, cp.wait_recv)

    def gather_second():
        for part in range(3):
            gather_wait(part, 0)
        for part in range(3):
            gather_start(part, 1)
        gather_start(0, 2, 0)
        gather_start(1, 2, 0)

        @pl.when(at.source)
        def _():
            gather_start(2, 2, 0)
            gather_start(2, 2, 1)

    def gather_third():
        for part in range(3):
            gather_wait(part, 1)

        @pl.when(at.other)
        def _():
            gather_start(2, 2, 0)

        gather_start(0, 2, 1)
        gather_start(1, 2, 1)

        @pl.when(at.other)
        def _():
            gather_start(2, 2, 1)

        for step in range(2, SPLIT):
            for part in range(3):
                gather_start(part, 2, step)

    @pl.when(at.source)
    def _():
        for part in range(3):
            ((start, _n),) = at.runs(part, 0)
            buf[0, start] = we_ref[part * ROWS : (part + 1) * ROWS]
            buf[1, start] = wc_ref[part * ROWS : (part + 1) * ROWS]

    for part in range(3):
        gather_start(part, 0)
    cot_copy = copy(cot_hbm, cot2.at[1], esem_s.at[0], esem_r.at[0], partner)
    cot_copy.start()

    pad[...] = jnp.zeros_like(pad)
    img_in.wait()

    def windows(values):
        pad[3:19, 8:24, :] = values.reshape(16, 16, 128)

    def conv_step(i, source, target, flip, finish):
        image, block = i // 6, i % 6
        lanes = pl.ds(pl.multiple_of(block * 128, 128), 128)
        windows(source[pl.ds(pl.multiple_of(image * 256, 256), 256), lanes].astype(F32))
        for half in range(2):
            acc = jnp.zeros((8, 16, 128), F32)
            for q in range(7):
                shifted = pad[half * 8 : half * 8 + 14, 5 + q : 21 + q, :]
                for p in range(7):
                    tap = 48 - (p * 7 + q) if flip else p * 7 + q
                    acc = acc + shifted[p : p + 8] * dwk_ref[tap // 7, tap % 7 : tap % 7 + 1, lanes].reshape(1, 1, 128)
            rows = pl.ds(pl.multiple_of(image * 256 + half * 128, 128), 128)
            target[rows, lanes] = finish(acc.reshape(128, 128), rows, lanes)

    def forward(i, carry):
        conv_step(i, img_ref, conv, False, lambda v, rows, lanes: v)

        @pl.when(i == 6)
        def _():
            gather_second()

        return carry

    lax.fori_loop(0, 12, forward, 0)

    def norm(i, carry):
        rows = pl.ds(pl.multiple_of(i * 64, 64), 64)
        v = conv[rows, :]
        centred = v - jnp.mean(v, axis=1, keepdims=True)
        istd = lax.rsqrt(jnp.mean(centred * centred, axis=1, keepdims=True) + EPSILON)
        nrm2[0, rows, :] = (centred * istd).astype(BF16)
        inv[rows, :] = jnp.broadcast_to(istd, (64, 128))
        mix[0, rows, :] = img_ref[rows, :].astype(F32)
        mix[1, rows, :] = jnp.zeros((64, C), F32)
        ngr[0, rows, :] = jnp.zeros((64, C), F32)
        ngr[1, rows, :] = jnp.zeros((64, C), F32)
        return carry

    lax.fori_loop(0, 8, norm, 0)
    nrm_copy = copy(nrm2.at[0], nrm2.at[1], esem_s.at[1], esem_r.at[1], partner)
    nrm_copy.start()
    gather_third()
    cot_in.wait()
    cot_copy.wait()
    nrm_copy.wait()

    def sides(part, phase):
        px = ORDERS[part].index("x")
        if phase < px:
            return (at.source,) * 4
        if phase == px:
            return at.other, at.source, at.source, at.source
        return (None,) * 4

    def reduce_last(part, step):
        axis = ORDERS[part][2]
        send_1, recv_1, send_2, recv_2 = sides(part, 2)
        share, count = at.share(part, step), sizes(part)[2] // SPLIT
        out = []
        for off, half, j in moves(axis):
            pieces = pl.ds(where(part, share, at.slot(axis, off)), count)
            lands = pl.ds(share * count, count)
            if half is None:
                a, b = grads.at[:, pieces], rbufs[part][2].at[j, :, lands]
            else:
                a, b = grads.at[half, pieces], rbufs[part][2].at[2, half, lands]
            cp = copy(a, b, rsem_s.at[part, 2, step, j], rsem_r.at[part, 2, step, j], at.peer(axis, off))
            out.append((cp, send_2 if j >= 2 else send_1, recv_2 if j >= 2 else recv_1))
        return out

    def reduce_middle(part, share, q):
        axis = ORDERS[part][1]
        send_1, recv_1, send_2, recv_2 = sides(part, 1)
        count = sizes(part)[2] // SPLIT
        per_block = sizes(part)[1] // count
        out = []
        for off, half, j in moves(axis):
            pieces, lands = pl.ds(share * count, count), pl.ds(q * count, count)
            src, dst = tbufs[part][2], rbufs[part][1]
            if half is None:
                a, b = src.at[:, pieces], dst.at[j, :, lands]
            else:
                a, b = src.at[half, pieces], dst.at[2, half, lands]
            cp = copy(a, b, rsem_s.at[part, 1, q, j], rsem_r.at[part, 1, q, j], at.peer(axis, off))
            goes = at.slot(axis, off) == share // per_block
            out.append((cp, goes, send_2 if j >= 2 else send_1, recv_2 if j >= 2 else recv_1))
        return out

    def reduce_first(part):
        axis = ORDERS[part][0]
        send_1, recv_1, send_2, recv_2 = sides(part, 0)
        out = []
        for off, half, j in moves(axis):
            pieces = pl.ds(at.slot(axis, off), 1)
            src, dst = tbufs[part][1], rbufs[part][0]
            if half is None:
                a, b = src.at[:, pieces], dst.at[j]
            else:
                a, b = src.at[half, pieces], dst.at[2, half]
            cp = copy(a, b, rsem_s.at[part, 0, 0, j], rsem_r.at[part, 0, 0, j], at.peer(axis, off))
            out.append((cp, send_2 if j >= 2 else send_1, recv_2 if j >= 2 else recv_1))
        return out

    def add_up(count, first, own, own_first, recv, dst):
        def piece(i, carry):
            for side in range(2):
                total = own[side, own_first + i].astype(F32) + recv[0, side, first + i].astype(F32)
                total = total + recv[1, side, first + i].astype(F32) + recv[2, side, first + i].astype(F32)
                dst[side, first + i] = total.astype(BF16)
            return carry

        lax.fori_loop(0, count, piece, 0)

    def reduce_start_last(step):
        for part in range(3):
            for cp, send_if, _ in reduce_last(part, step):
                when(send_if, cp.start)

    def reduce_second(step):
        for part in range(3):
            for cp, send_if, recv_if in reduce_last(part, step):
                when(send_if, cp.wait_send)
                when(recv_if, cp.wait_recv)
            share, count = at.share(part, step), sizes(part)[2] // SPLIT
            per_block = sizes(part)[1] // count

            def go(part=part, share=share, count=count, per_block=per_block):
                mine = where(part, share, at.slot(ORDERS[part][2]))
                add_up(count, share * count, grads, mine, rbufs[part][2], tbufs[part][2])
                for cp, goes, send_if, _ in reduce_middle(part, share, share % per_block):
                    when(goes if send_if is None else jnp.logical_and(goes, send_if), cp.start)

            when(at.source if ORDERS[part][2] == "x" else None, go)

    def reduce_third():
        for part in range(3):
            count = sizes(part)[2] // SPLIT
            per_block = sizes(part)[1] // count
            for q in range(per_block):
                for cp, _, send_if, recv_if in reduce_middle(part, q, q):
                    when(send_if, cp.wait_send)
                    when(recv_if, cp.wait_recv)

            def go(part=part):
                n1 = sizes(part)[1]
                add_up(n1, 0, tbufs[part][2], at.slot(ORDERS[part][1]) * n1, rbufs[part][1], tbufs[part][1])

            when(at.source if ORDERS[part].index("x") >= 1 else None, go)
            for cp, send_if, _ in reduce_first(part):
                when(send_if, cp.start)

    def reduce_end():
        for part in range(3):
            for cp, send_if, recv_if in reduce_first(part):
                when(send_if, cp.wait_send)
                when(recv_if, cp.wait_recv)

            def go(part=part):
                add_up(1, 0, tbufs[part][1], at.slot(ORDERS[part][0]), rbufs[part][0], tbufs[part][0])

            when(at.source, go)

    count = 32 // SPLIT
    width = 3 * count * ROWS

    def share_step(step, carry):
        for part in range(3):
            gather_wait(part, 2, step)
        normed = nrm2[...].reshape(2 * TOK, C)
        upstream = cot2[...].reshape(2 * TOK, C)
        here = [pl.ds(where(part, at.share(part, step), 0), count) for part in range(3)]
        expand = jnp.concatenate([buf[0, h] for h in here]).reshape(width, C)
        contract = jnp.concatenate([buf[1, h] for h in here]).reshape(width, C)
        pre_act = dot(normed, expand, NT)
        act_grad = dot(upstream, contract, NT)
        cdf = 0.5 * (1.0 + lax.erf(pre_act * SQRT_HALF))
        activated = (pre_act * cdf).astype(BF16)
        slope = cdf + pre_act * jnp.exp(-0.5 * pre_act * pre_act) * INV_ROOT_TWO_PI
        pre_grad = (act_grad * slope).astype(BF16)
        grad_e = dot(pre_grad, normed, TN).astype(BF16).reshape(3, count, ROWS, C)
        grad_c = dot(activated, upstream, TN).astype(BF16).reshape(3, count, ROWS, C)
        for part in range(3):
            grads[0, here[part]] = grad_e[part]
            grads[1, here[part]] = grad_c[part]
        reduce_start_last(step)
        ngr[...] += dot(pre_grad, expand, NN).reshape(2, TOK, C)
        mix[...] += dot(activated, contract, NN).reshape(2, TOK, C)

        @pl.when(step >= 2)
        def _():
            reduce_second(step - 2)

        return carry

    lax.fori_loop(0, SPLIT, share_step, 0)
    def send_back(i, source):
        def to_send(k, carry):
            rows = pl.ds(pl.multiple_of(k * 64, 64), 64)
            ex_send[i, rows, :] = source[1, rows, :].astype(BF16)
            return carry

        lax.fori_loop(0, 8, to_send, 0)
        cp = copy(ex_send.at[i], ex_recv.at[i], esem_s.at[2 + i], esem_r.at[2 + i], partner)
        cp.start()
        return cp

    ngr_copy = send_back(0, ngr)
    mix_copy = send_back(1, mix)
    ngr_copy.wait()
    def norm_back(i, carry):
        rows = pl.ds(pl.multiple_of(i * 64, 64), 64)
        grad = ngr[0, rows, :] + ex_recv[0, rows, :].astype(F32)
        standard = nrm2[0, rows, :].astype(F32)
        mean = jnp.mean(grad, axis=1, keepdims=True)
        along = jnp.mean(grad * standard, axis=1, keepdims=True)
        conv[rows, :] = inv[rows, 0:1] * (grad - mean - standard * along)
        return carry

    lax.fori_loop(0, 8, norm_back, 0)

    def kernel_terms(block, carry):
        @pl.when(block % 3 == 0)
        def _():
            reduce_second(2 + block // 3)

        lanes = pl.ds(pl.multiple_of(block * 128, 128), 128)
        for image in range(2):
            windows(img_ref[image * 256 : image * 256 + 256, lanes].astype(F32))
            for half in range(2):
                first = image * 256 + half * 128
                g = conv[first : first + 128, lanes].reshape(8, 16, 128)
                for q in range(7):
                    shifted = pad[half * 8 : half * 8 + 14, 5 + q : 21 + q, :]
                    for p in range(7):
                        r = jnp.sum((g * shifted[p : p + 8]).reshape(16, 8, 128), axis=0)
                        if image == 0 and half == 0:
                            kacc[p * 7 + q, :, lanes] = r
                        else:
                            kacc[p * 7 + q, :, lanes] += r
        return carry

    lax.fori_loop(0, 6, kernel_terms, 0)
    kall[49:64, :] = jnp.zeros((15, C), F32)
    kall[0:49, :] = jnp.sum(kacc[...], axis=1)

    plane = [(0, 1 - at.core)] + [(off, core) for off in (1, -1, 2) for core in (at.core, 1 - at.core)]

    def kx_copies():
        out = []
        for j, (off, core) in enumerate(plane):
            rows = pl.ds(core * 32 + ((at.x + off + 4) % 4) * 8, 8)
            out.append(copy(kall.at[rows], krx.at[j], ksem_s.at[j], ksem_r.at[j], at.peer("x", off, core)))
        return out

    def ky_copies():
        return [
            copy(ky.at[at.y], ky.at[at.y], ksem_s.at[7 + j], ksem_r.at[7 + j], at.peer("y", off))
            for j, off in enumerate((1, -1, 2))
        ]

    def kz_copies():
        return [
            copy(kz.at[at.z], kz.at[at.z], ksem_s.at[10 + j], ksem_r.at[10 + j], at.peer("z", off))
            for j, off in enumerate(range(1, 8))
        ]

    share = pl.ds(at.core * 32 + at.x * 8, 8)

    def kg_copies():
        return [
            copy(finf.at[share], finf.at[share], ksem_s.at[17 + j], ksem_r.at[17 + j], at.peer("x", off, core))
            for j, (off, core) in enumerate(plane)
        ]

    def start_all(copies):
        for cp in copies:
            cp.start()

    def wait_all(copies):
        for cp in copies:
            cp.wait()

    start_all(kx_copies())
    mix_copy.wait()

    def block_out(i, carry):
        rows = pl.ds(pl.multiple_of(i * 64, 64), 64)
        out_ref[rows, :] = (mix[0, rows, :] + ex_recv[1, rows, :].astype(F32)).astype(BF16)
        return carry

    lax.fori_loop(0, 8, block_out, 0)
    block_copy = pltpu.make_async_copy(out_ref, out_hbm, lsem.at[2])
    block_copy.start()

    scale = float(TOK * 256) ** (-0.5)

    far = at.peer("z", 4)

    def far_copy():
        return copy(fin.at[at.hi], fin.at[at.hi], fsem_s.at[0], fsem_r.at[0], far)

    def near_copies():
        return [
            copy(ge_ref, ge_ref, fsem_s.at[1], fsem_r.at[1], partner),
            copy(gc_ref, gc_ref, fsem_s.at[2], fsem_r.at[2], partner),
        ]

    def far_start():
        @pl.when(at.source)
        def _():
            for part in range(3):
                for side in range(2):
                    fin[at.hi, side, part] = tbufs[part][0][side, 0]
            far_copy().start()

    def backward(i, carry):
        conv_step(
            i, conv, gimg_ref, True,
            lambda v, rows, lanes: (v + cot2[0, rows, lanes].astype(F32)).astype(BF16),
        )

        @pl.when(i == 0)
        def _():
            reduce_third()

        @pl.when(i == 3)
        def _():
            wait_all(kx_copies())
            total = kall[pl.ds(pl.multiple_of(at.core * 32 + at.x * 8, 8), 8), :]
            for j in range(7):
                total = total + krx[j]
            ky[at.y] = total
            start_all(ky_copies())

        @pl.when(i == 9)
        def _():
            wait_all(ky_copies())
            kz[at.z] = ky[0] + ky[1] + ky[2] + ky[3]
            start_all(kz_copies())
            reduce_end()
            far_start()

        return carry

    lax.fori_loop(0, 12, backward, 0)
    gimg_copy = pltpu.make_async_copy(gimg_ref, gimg_hbm, lsem.at[3])
    gimg_copy.start()
    wait_all(kz_copies())
    total = kz[0]
    for i in range(1, 8):
        total = total + kz[i]
    finf[pl.ds(pl.multiple_of(at.core * 32 + at.x * 8, 8), 8), :] = total
    start_all(kg_copies())

    @pl.when(at.source)
    def _():
        far_copy().wait()
        for side, ref in ((0, ge_ref), (1, gc_ref)):
            for part in range(3):
                total = fin[0, side, part].astype(F32) + fin[1, side, part].astype(F32)
                ref[part * ROWS : (part + 1) * ROWS, :] = total * scale
        for cp in near_copies():
            cp.start()

    wait_all(kg_copies())
    for i in range(7):
        gker_ref[i] = finf[7 * i : 7 * i + 7, :] * scale

    @pl.when(at.source)
    def _():
        for cp in near_copies():
            cp.wait_send()

    @pl.when(at.other)
    def _():
        for cp in near_copies():
            cp.wait_recv()

    block_copy.wait()
    gimg_copy.wait()


def hand_over(*refs):
    n = len(refs) // 3
    sem = refs[-1]
    loads = [pltpu.make_async_copy(refs[i], refs[2 * n + i], sem.at[0, i]) for i in range(n)]
    stores = [pltpu.make_async_copy(refs[2 * n + i], refs[n + i], sem.at[1, i]) for i in range(n)]
    for cp in loads:
        cp.start()
    for load, store in zip(loads, stores):
        load.wait()
        store.start()
    for cp in stores:
        cp.wait()


def per_device(images, cotangent, dw_kernel, w_expand, w_contract):
    vmem = lambda: pl.BlockSpec(memory_space=pltpu.VMEM)
    anywhere = lambda: pl.BlockSpec(memory_space=pl.ANY)
    scratch = [
        pltpu.VMEM((TOK, C), BF16),
        pltpu.VMEM((TOK, C), BF16),
        pltpu.VMEM((TOK, C), BF16),
        pltpu.VMEM((2, 96, ROWS, C), BF16),
        pltpu.VMEM((2, 96, ROWS, C), BF16),
        pltpu.VMEM((2, TOK, C), BF16),
        pltpu.VMEM((2, TOK, C), BF16),
        pltpu.VMEM((2, TOK, C), F32),
        pltpu.VMEM((2, TOK, C), F32),
        pltpu.VMEM((2, TOK, C), BF16),
        pltpu.VMEM((2, TOK, C), BF16),
        pltpu.VMEM((TOK, C), F32),
        pltpu.VMEM((TOK, 128), F32),
        pltpu.VMEM((22, 32, 128), F32),
        pltpu.VMEM((49, 8, C), F32),
        pltpu.VMEM((64, C), F32),
                pltpu.VMEM((7, 8, C), F32),
        pltpu.VMEM((4, 8, C), F32),
        pltpu.VMEM((8, 8, C), F32),
        pltpu.VMEM((2, 2, 3, ROWS, C), BF16),
        pltpu.VMEM((64, C), F32),
    ]
    for part in range(3):
        for phase in range(3):
            scratch.append(pltpu.VMEM((3, 2, sizes(part)[phase], ROWS, C), BF16))
    for part in range(3):
        for phase in range(3):
            scratch.append(pltpu.VMEM((2, sizes(part)[phase], ROWS, C), BF16))
    scratch += [pltpu.SemaphoreType.DMA((3, 3, SPLIT, 4))] * 4
    scratch += [pltpu.SemaphoreType.DMA((4,))] * 2
    scratch += [pltpu.SemaphoreType.DMA((24,))] * 2
    scratch += [pltpu.SemaphoreType.DMA((3,))] * 2
    scratch += [pltpu.SemaphoreType.DMA((4,))]
    shapes = (
        jax.ShapeDtypeStruct((TOK, C), BF16),
        jax.ShapeDtypeStruct((TOK, C), BF16),
        jax.ShapeDtypeStruct((7, 7, C), F32),
        jax.ShapeDtypeStruct((48, C), F32),
        jax.ShapeDtypeStruct((48, C), F32),
    )
    results = pl.pallas_call(
        kernel,
        name="block_step",
        out_shape=shapes,
        in_specs=[anywhere(), anywhere(), vmem(), vmem(), vmem()],
        out_specs=(anywhere(), anywhere(), vmem(), vmem(), vmem()),
        scratch_shapes=scratch,
        compiler_params=pltpu.CompilerParams(
            collective_id=0, has_side_effects=True, vmem_limit_bytes=60 * 2**20
        ),
        cost_estimate=pl.CostEstimate(flops=15 * 10**9, bytes_accessed=10**7, transcendentals=10**6),
    )(
        images.reshape(TOK, C),
        cotangent.reshape(TOK, C),
        dw_kernel,
        w_expand,
        w_contract,
    )
    out, gimg, gker, ge, gc = pl.pallas_call(
        hand_over,
        name="hand_over",
        out_shape=shapes,
        in_specs=[anywhere() for _ in range(5)],
        out_specs=tuple(anywhere() for _ in range(5)),
        scratch_shapes=[pltpu.VMEM(a.shape, a.dtype) for a in shapes] + [pltpu.SemaphoreType.DMA((2, 5))],
    )(*results)
    return out.reshape(images.shape), gimg.reshape(images.shape), gker, ge, gc


def solution(mesh):
    tokens = P(("grp", "dev"), None, None, None)
    rows = P("dev", None)
    return jax.shard_map(
        per_device,
        mesh=mesh,
        in_specs=(tokens, tokens, P(), rows, rows),
        out_specs=(tokens, tokens, P(), rows, rows),
        check_vma=False,
    )
```

```python
import functools

import jax
import jax.numpy as jnp
from jax import lax
from jax.experimental import pallas as pl
from jax.experimental.pallas import tpu as pltpu
from jax.sharding import PartitionSpec as P

MESH = pl.DeviceIdType.MESH
F32, BF16 = jnp.float32, jnp.bfloat16
SQRT_HALF = 0.7071067811865476
INV_ROOT_TWO_PI = 0.3989422804014327
EPSILON = 1e-06
NT = (((1,), (1,)), ((), ()))
NN = (((1,), (0,)), ((), ()))
TN = (((0,), (0,)), ((), ()))

C = 768
TOK = 512
ROWS = 16
SPLIT = 4
ORDERS = (("x", "y", "z"), ("y", "z", "x"), ("z", "x", "y"))
SIZE = {"x": 2, "y": 4, "z": 4}


def dot(a, b, dims):
    return lax.dot_general(a, b, dims, preferred_element_type=F32)


def sizes(part):
    n = [SIZE[a] for a in ORDERS[part]]
    return (1, n[0], n[0] * n[1])


class Place:
    def __init__(self):
        grp, dev = lax.axis_index("grp"), lax.axis_index("dev")
        self.hi, self.core = grp // 2, grp % 2
        self.y, self.zlo, self.x = dev // 16, (dev // 4) % 4, dev % 4
        self.z = self.hi * 4 + self.zlo
        self.source = (self.x % 2) == self.core
        self.other = (self.x % 2) != self.core

    def device(self, x, y, z, core):
        return {"grp": (z // 4) * 2 + core, "dev": (y * 4 + z % 4) * 4 + x}

    def peer(self, axis, off, core=None):
        core = self.core if core is None else core
        x, y, z = self.x, self.y, self.z
        if axis == "x":
            x = (x + off + 4) % 4
        elif axis == "y":
            y = (y + off + 4) % 4
        else:
            z = (z + off + 8) % 8
        return self.device(x, y, z, core)

    def slot(self, axis, off=0):
        if axis == "x":
            return ((self.x + off + 4) % 4) // 2
        if axis == "y":
            return (self.y + off + 4) % 4
        return (self.zlo + off + 4) % 4

    def share(self, part, step):
        first = (self.y, self.zlo, 2 * (self.x // 2))[part]
        return (first + step) % SPLIT

    def runs(self, part, phase):
        order = ORDERS[part]
        n = [SIZE[a] for a in order]
        i = [self.slot(a) for a in order]
        share = n[0] * n[1] // SPLIT
        if phase == 1:
            first, count = i[1] * n[0], n[0]
        else:
            first, count = i[1] * n[0] + i[0], 1
        step = min(count, share)
        return [
            (where(part, (first + k) // share, i[2]) + (first + k) % share, step)
            for k in range(0, count, step)
        ]


def where(part, s, i3):
    share = sizes(part)[2] // SPLIT
    return s * (96 // SPLIT) + part * (32 // SPLIT) + i3 * share


def moves(axis):
    if axis == "z":
        return ((1, None, 0), (-1, None, 1), (2, 0, 2), (-2, 1, 3))
    return ((1, None, 0), (-1, None, 1), (2, None, 2))


def when(cond, fn):
    if cond is None:
        fn()
    else:
        pl.when(cond)(fn)


def kernel(
    img_hbm, cot_hbm, dwk_ref, we_ref, wc_ref,
    out_hbm, gimg_hbm, gker_ref, ge_ref, gc_ref,
    img_ref, out_ref, gimg_ref, buf, grads, nrm2, cot2, mix, ngr, ex_send, ex_recv, conv, inv, pad, kacc,
    kall, krx, ky, kz, fin, finf, acts,
    rb0, rb1, rb2, rb3, rb4, rb5, rb6, rb7, rb8,
    t0, t1, t2, t3, t4, t5, t6, t7, t8,
    bsem_s, bsem_r, rsem_s, rsem_r, esem_s, esem_r, ksem_s, ksem_r, fsem_s, fsem_r, lsem,
):
    rbufs = ((rb0, rb1, rb2), (rb3, rb4, rb5), (rb6, rb7, rb8))
    tbufs = ((t0, t1, t2), (t3, t4, t5), (t6, t7, t8))
    at = Place()
    partner = at.device(at.x, at.y, at.z, 1 - at.core)

    barrier = pltpu.get_barrier_semaphore()
    friends = [at.peer("x", o) for o in (1, -1, 2)] + [at.peer("y", o) for o in (1, -1, 2)]
    friends += [at.peer("z", o) for o in range(1, 8)] + [partner]
    friends += [at.peer("x", o, 1 - at.core) for o in (1, -1, 2)]
    for friend in friends:
        pl.semaphore_signal(barrier, inc=1, device_id=friend, device_id_type=MESH)
    quarters = [pl.ds(i * 128, 128) for i in range(4)]
    img_in = [pltpu.make_async_copy(img_hbm.at[q], img_ref.at[q], lsem.at[0, i]) for i, q in enumerate(quarters)]
    cot_in = [pltpu.make_async_copy(cot_hbm.at[q], cot2.at[0, q], lsem.at[1, i]) for i, q in enumerate(quarters)]
    for cp in img_in + cot_in:
        cp.start()
    pl.semaphore_wait(barrier, len(friends))

    def copy(src, dst, send, recv, to):
        return pltpu.make_async_remote_copy(
            src_ref=src, dst_ref=dst, send_sem=send, recv_sem=recv,
            device_id=to, device_id_type=MESH,
        )

    def gather_copies(part, phase, step=None, kind=None):
        axis = ORDERS[part][phase]
        px = ORDERS[part].index("x")
        if phase == 2:
            share, count = at.share(part, step), sizes(part)[2] // SPLIT
            runs = [(step, (where(part, share, at.slot(axis)), count))]
        else:
            runs = enumerate(at.runs(part, phase))
        if kind == "pass":
            out = []
            for off, half, j in ((1, 0, 2), (-1, 1, 3)):
                ref = buf.at[half, pl.ds(where(part, share, at.slot(axis, -off)), count)]
                cp = copy(ref, ref, bsem_s.at[part, phase, step, j], bsem_r.at[part, phase, step, j], at.peer(axis, off))
                out.append((cp, at.other if axis == "x" else None, at.source if axis == "x" else None))
            return out
        out = []
        for r, (start, count) in runs:
            for off, half, j in moves(axis)[: 2 if kind == "near" else 4]:
                if half is None:
                    ref = buf.at[:, pl.ds(start, count)]
                else:
                    ref = buf.at[half, pl.ds(start, count)]
                cp = copy(ref, ref, bsem_s.at[part, phase, r, j], bsem_r.at[part, phase, r, j], at.peer(axis, off))
                if phase < px:
                    send_if = recv_if = at.source
                elif phase == px:
                    send_if = at.source
                    recv_if = at.source if j == 2 else at.other
                else:
                    send_if = recv_if = None
                out.append((cp, send_if, recv_if))
        return out

    def gather_start(part, phase, step=None, kind=None):
        for cp, send_if, _ in gather_copies(part, phase, step, kind):
            when(send_if, cp.start)

    def gather_wait(part, phase, step=None, kind=None):
        for cp, send_if, recv_if in gather_copies(part, phase, step, kind):
            when(send_if, cp.wait_send)
            when(recv_if, cp.wait_recv)

    def gather_second():
        for part in range(3):
            gather_wait(part, 0)
        for part in range(3):
            gather_start(part, 1)
        gather_start(0, 2, 0)
        gather_start(1, 2, 0)

        @pl.when(at.source)
        def _():
            gather_start(2, 2, 0)
            gather_start(2, 2, 1, "near")

    def gather_third():
        for part in range(3):
            gather_wait(part, 1)

        @pl.when(at.other)
        def _():
            gather_start(2, 2, 0)

        gather_start(0, 2, 1, "near")
        gather_start(1, 2, 1, "near")

        @pl.when(at.other)
        def _():
            gather_start(2, 2, 1, "near")

        for step in range(2, SPLIT):
            for part in range(3):
                gather_start(part, 2, step, "near")

    def gather_pass(step):
        for part in range(3):
            gather_wait(part, 2, step, "near")
            gather_start(part, 2, step, "pass")

    @pl.when(at.source)
    def _():
        for part in range(3):
            ((start, _n),) = at.runs(part, 0)
            buf[0, start] = we_ref[part * ROWS : (part + 1) * ROWS]
            buf[1, start] = wc_ref[part * ROWS : (part + 1) * ROWS]

    for part in range(3):
        gather_start(part, 0)
    cot_copy = copy(cot_hbm, cot2.at[1], esem_s.at[0], esem_r.at[0], partner)
    cot_copy.start()

    pad[...] = jnp.zeros_like(pad)
    for cp in img_in:
        cp.wait()

    def windows(values):
        pad[3:19, 8:24, :] = values.reshape(16, 16, 128)

    def conv_step(i, source, target, flip, finish):
        image, block = i // 6, i % 6
        lanes = pl.ds(pl.multiple_of(block * 128, 128), 128)
        windows(source[pl.ds(pl.multiple_of(image * 256, 256), 256), lanes].astype(F32))
        for half in range(2):
            acc = jnp.zeros((8, 16, 128), F32)
            for q in range(7):
                shifted = pad[half * 8 : half * 8 + 14, 5 + q : 21 + q, :]
                for p in range(7):
                    tap = 48 - (p * 7 + q) if flip else p * 7 + q
                    acc = acc + shifted[p : p + 8] * dwk_ref[tap // 7, tap % 7 : tap % 7 + 1, lanes].reshape(1, 1, 128)
            rows = pl.ds(pl.multiple_of(image * 256 + half * 128, 128), 128)
            target[rows, lanes] = finish(acc.reshape(128, 128), rows, lanes)

    def forward(i, carry):
        conv_step(i, img_ref, conv, False, lambda v, rows, lanes: v)

        @pl.when(i == 6)
        def _():
            gather_second()

        return carry

    lax.fori_loop(0, 12, forward, 0)

    def norm(i, carry):
        rows = pl.ds(pl.multiple_of(i * 64, 64), 64)
        v = conv[rows, :]
        centred = v - jnp.mean(v, axis=1, keepdims=True)
        istd = lax.rsqrt(jnp.mean(centred * centred, axis=1, keepdims=True) + EPSILON)
        nrm2[0, rows, :] = (centred * istd).astype(BF16)
        inv[rows, :] = jnp.broadcast_to(istd, (64, 128))
        mix[0, rows, :] = img_ref[rows, :].astype(F32)
        mix[1, rows, :] = jnp.zeros((64, C), F32)
        ngr[0, rows, :] = jnp.zeros((64, C), F32)
        ngr[1, rows, :] = jnp.zeros((64, C), F32)
        return carry

    lax.fori_loop(0, 8, norm, 0)
    nrm_copy = copy(nrm2.at[0], nrm2.at[1], esem_s.at[1], esem_r.at[1], partner)
    nrm_copy.start()
    gather_third()
    for cp in cot_in:
        cp.wait()
    cot_copy.wait()
    nrm_copy.wait()

    def sides(part, phase):
        px = ORDERS[part].index("x")
        if phase < px:
            return (at.source,) * 4
        if phase == px:
            return at.other, at.source, at.source, at.source
        return (None,) * 4

    def reduce_last(part, step):
        axis = ORDERS[part][2]
        send_1, recv_1, send_2, recv_2 = sides(part, 2)
        share, count = at.share(part, step), sizes(part)[2] // SPLIT
        out = []
        for off, half, j in moves(axis):
            pieces = pl.ds(where(part, share, at.slot(axis, off)), count)
            lands = pl.ds(share * count, count)
            if half is None:
                a, b = grads.at[:, pieces], rbufs[part][2].at[j, :, lands]
            else:
                a, b = grads.at[half, pieces], rbufs[part][2].at[2, half, lands]
            cp = copy(a, b, rsem_s.at[part, 2, step, j], rsem_r.at[part, 2, step, j], at.peer(axis, off))
            out.append((cp, send_2 if j >= 2 else send_1, recv_2 if j >= 2 else recv_1))
        return out

    def reduce_middle(part, share, q):
        axis = ORDERS[part][1]
        send_1, recv_1, send_2, recv_2 = sides(part, 1)
        count = sizes(part)[2] // SPLIT
        per_block = sizes(part)[1] // count
        out = []
        for off, half, j in moves(axis):
            pieces, lands = pl.ds(share * count, count), pl.ds(q * count, count)
            src, dst = tbufs[part][2], rbufs[part][1]
            if half is None:
                a, b = src.at[:, pieces], dst.at[j, :, lands]
            else:
                a, b = src.at[half, pieces], dst.at[2, half, lands]
            cp = copy(a, b, rsem_s.at[part, 1, q, j], rsem_r.at[part, 1, q, j], at.peer(axis, off))
            goes = at.slot(axis, off) == share // per_block
            out.append((cp, goes, send_2 if j >= 2 else send_1, recv_2 if j >= 2 else recv_1))
        return out

    def reduce_first(part):
        axis = ORDERS[part][0]
        send_1, recv_1, send_2, recv_2 = sides(part, 0)
        out = []
        for off, half, j in moves(axis):
            pieces = pl.ds(at.slot(axis, off), 1)
            src, dst = tbufs[part][1], rbufs[part][0]
            if half is None:
                a, b = src.at[:, pieces], dst.at[j]
            else:
                a, b = src.at[half, pieces], dst.at[2, half]
            cp = copy(a, b, rsem_s.at[part, 0, 0, j], rsem_r.at[part, 0, 0, j], at.peer(axis, off))
            out.append((cp, send_2 if j >= 2 else send_1, recv_2 if j >= 2 else recv_1))
        return out

    def add_up(count, first, own, own_first, recv, dst):
        def piece(i, carry):
            for side in range(2):
                total = own[side, own_first + i].astype(F32) + recv[0, side, first + i].astype(F32)
                total = total + recv[1, side, first + i].astype(F32) + recv[2, side, first + i].astype(F32)
                dst[side, first + i] = total.astype(BF16)
            return carry

        lax.fori_loop(0, count, piece, 0)

    def reduce_start_last(step):
        for part in range(3):
            for cp, send_if, _ in reduce_last(part, step):
                when(send_if, cp.start)

    def reduce_second(step):
        for part in range(3):
            for cp, send_if, recv_if in reduce_last(part, step):
                when(send_if, cp.wait_send)
                when(recv_if, cp.wait_recv)
            share, count = at.share(part, step), sizes(part)[2] // SPLIT
            per_block = sizes(part)[1] // count

            def go(part=part, share=share, count=count, per_block=per_block):
                mine = where(part, share, at.slot(ORDERS[part][2]))
                add_up(count, share * count, grads, mine, rbufs[part][2], tbufs[part][2])
                for cp, goes, send_if, _ in reduce_middle(part, share, share % per_block):
                    when(goes if send_if is None else jnp.logical_and(goes, send_if), cp.start)

            when(at.source if ORDERS[part][2] == "x" else None, go)

    def reduce_third():
        for part in range(3):
            count = sizes(part)[2] // SPLIT
            per_block = sizes(part)[1] // count
            for q in range(per_block):
                for cp, _, send_if, recv_if in reduce_middle(part, q, q):
                    when(send_if, cp.wait_send)
                    when(recv_if, cp.wait_recv)

            def go(part=part):
                n1 = sizes(part)[1]
                add_up(n1, 0, tbufs[part][2], at.slot(ORDERS[part][1]) * n1, rbufs[part][1], tbufs[part][1])

            when(at.source if ORDERS[part].index("x") >= 1 else None, go)
            for cp, send_if, _ in reduce_first(part):
                when(send_if, cp.start)

    def reduce_end():
        for part in range(3):
            for cp, send_if, recv_if in reduce_first(part):
                when(send_if, cp.wait_send)
                when(recv_if, cp.wait_recv)

            def go(part=part):
                add_up(1, 0, tbufs[part][1], at.slot(ORDERS[part][0]), rbufs[part][0], tbufs[part][0])

            when(at.source, go)

    count = 32 // SPLIT
    width = 3 * count * ROWS

    def mix_step(step, carry):
        here = [pl.ds(where(part, at.share(part, step), 0), count) for part in range(3)]
        contract = jnp.concatenate([buf[1, h] for h in here]).reshape(width, C)
        mix[...] += dot(acts[step], contract, NN).reshape(2, TOK, C)
        return carry

    for part in range(3):
        gather_wait(part, 2, 0)

    def share_step(step, carry):
        @pl.when(step == 1)
        def _():
            gather_pass(2)

        @pl.when(step >= 1)
        def _():
            for part in range(3):
                gather_wait(part, 2, step, "pass")

        normed = nrm2[...].reshape(2 * TOK, C)
        upstream = cot2[...].reshape(2 * TOK, C)
        here = [pl.ds(where(part, at.share(part, step), 0), count) for part in range(3)]
        expand = jnp.concatenate([buf[0, h] for h in here]).reshape(width, C)
        contract = jnp.concatenate([buf[1, h] for h in here]).reshape(width, C)
        pre_act = dot(normed, expand, NT)
        act_grad = dot(upstream, contract, NT)
        cdf = 0.5 * (1.0 + lax.erf(pre_act * SQRT_HALF))
        activated = (pre_act * cdf).astype(BF16)
        slope = cdf + pre_act * jnp.exp(-0.5 * pre_act * pre_act) * INV_ROOT_TWO_PI
        pre_grad = (act_grad * slope).astype(BF16)
        grad_e = dot(pre_grad, normed, TN).astype(BF16).reshape(3, count, ROWS, C)
        grad_c = dot(activated, upstream, TN).astype(BF16).reshape(3, count, ROWS, C)
        for part in range(3):
            grads[0, here[part]] = grad_e[part]
            grads[1, here[part]] = grad_c[part]
        acts[step] = activated

        @pl.when(step <= 1)
        def _():
            gather_pass(2 * step + 1)

        reduce_start_last(step)
        ngr[...] += dot(pre_grad, expand, NN).reshape(2, TOK, C)

        @pl.when(step >= 2)
        def _():
            reduce_second(step - 2)

        return carry

    lax.fori_loop(0, SPLIT, share_step, 0)
    def send_back(i, source):
        def to_send(k, carry):
            rows = pl.ds(pl.multiple_of(k * 64, 64), 64)
            ex_send[i, rows, :] = source[1, rows, :].astype(BF16)
            return carry

        lax.fori_loop(0, 8, to_send, 0)
        cp = copy(ex_send.at[i], ex_recv.at[i], esem_s.at[2 + i], esem_r.at[2 + i], partner)
        cp.start()
        return cp

    ngr_copy = send_back(0, ngr)

    lax.fori_loop(0, 2, mix_step, 0)
    ngr_copy.wait()
    def norm_back(i, carry):
        rows = pl.ds(pl.multiple_of(i * 64, 64), 64)
        grad = ngr[0, rows, :] + ex_recv[0, rows, :].astype(F32)
        standard = nrm2[0, rows, :].astype(F32)
        mean = jnp.mean(grad, axis=1, keepdims=True)
        along = jnp.mean(grad * standard, axis=1, keepdims=True)
        conv[rows, :] = inv[rows, 0:1] * (grad - mean - standard * along)
        return carry

    lax.fori_loop(0, 8, norm_back, 0)

    def kernel_terms(block, carry):
        @pl.when(jnp.logical_or(block == 0, block == 4))
        def _():
            reduce_second(2 + block // 4)

        lanes = pl.ds(pl.multiple_of(block * 128, 128), 128)
        for image in range(2):
            windows(img_ref[image * 256 : image * 256 + 256, lanes].astype(F32))
            for half in range(2):
                first = image * 256 + half * 128
                g = conv[first : first + 128, lanes].reshape(8, 16, 128)
                for q in range(7):
                    shifted = pad[half * 8 : half * 8 + 14, 5 + q : 21 + q, :]
                    for p in range(7):
                        r = jnp.sum((g * shifted[p : p + 8]).reshape(16, 8, 128), axis=0)
                        if image == 0 and half == 0:
                            kacc[p * 7 + q, :, lanes] = r
                        else:
                            kacc[p * 7 + q, :, lanes] += r
        return carry

    lax.fori_loop(0, 6, kernel_terms, 0)
    kall[49:64, :] = jnp.zeros((15, C), F32)
    kall[0:49, :] = jnp.sum(kacc[...], axis=1)

    plane = [(0, 1 - at.core)] + [(off, core) for off in (1, -1, 2) for core in (at.core, 1 - at.core)]

    def kx_copies():
        out = []
        for j, (off, core) in enumerate(plane):
            rows = pl.ds(core * 32 + ((at.x + off + 4) % 4) * 8, 8)
            out.append(copy(kall.at[rows], krx.at[j], ksem_s.at[j], ksem_r.at[j], at.peer("x", off, core)))
        return out

    def ky_copies():
        return [
            copy(ky.at[at.y], ky.at[at.y], ksem_s.at[7 + j], ksem_r.at[7 + j], at.peer("y", off))
            for j, off in enumerate((1, -1, 2))
        ]

    def kz_copies():
        return [
            copy(kz.at[at.z], kz.at[at.z], ksem_s.at[10 + j], ksem_r.at[10 + j], at.peer("z", off))
            for j, off in enumerate(range(1, 8))
        ]

    share = pl.ds(at.core * 32 + at.x * 8, 8)

    def kg_copies():
        return [
            copy(finf.at[share], finf.at[share], ksem_s.at[17 + j], ksem_r.at[17 + j], at.peer("x", off, core))
            for j, (off, core) in enumerate(plane)
        ]

    def start_all(copies):
        for cp in copies:
            cp.start()

    def wait_all(copies):
        for cp in copies:
            cp.wait()

    start_all(kx_copies())

    scale = float(TOK * 256) ** (-0.5)

    far = at.peer("z", 4)

    def far_copy():
        return copy(fin.at[at.hi], fin.at[at.hi], fsem_s.at[0], fsem_r.at[0], far)

    def near_copy(half):
        return copy(fin.at[half], fin.at[half], fsem_s.at[half + 1], fsem_r.at[half + 1], partner)

    def far_start():
        @pl.when(at.source)
        def _():
            for part in range(3):
                for side in range(2):
                    fin[at.hi, side, part] = tbufs[part][0][side, 0]
            far_copy().start()
            near_copy(at.hi).start()

    def backward(i, carry):
        conv_step(
            i, conv, gimg_ref, True,
            lambda v, rows, lanes: (v + cot2[0, rows, lanes].astype(F32)).astype(BF16),
        )

        @pl.when(i == 5)
        def _():
            reduce_third()

        @pl.when(i == 6)
        def _():
            wait_all(kx_copies())
            total = kall[pl.ds(pl.multiple_of(at.core * 32 + at.x * 8, 8), 8), :]
            for j in range(7):
                total = total + krx[j]
            ky[at.y] = total
            start_all(ky_copies())

        return carry

    lax.fori_loop(0, 12, backward, 0)
    gimg_copy = pltpu.make_async_copy(gimg_ref, gimg_hbm, lsem.at[3, 0])
    gimg_copy.start()
    mix_step(2, 0)
    wait_all(ky_copies())
    kz[at.z] = ky[0] + ky[1] + ky[2] + ky[3]
    start_all(kz_copies())
    reduce_end()
    far_start()
    mix_step(3, 0)
    mix_copy = send_back(1, mix)
    wait_all(kz_copies())
    total = kz[0]
    for i in range(1, 8):
        total = total + kz[i]
    finf[pl.ds(pl.multiple_of(at.core * 32 + at.x * 8, 8), 8), :] = total
    start_all(kg_copies())
    mix_copy.wait()

    def block_out(i, carry):
        rows = pl.ds(pl.multiple_of(i * 64, 64), 64)
        out_ref[rows, :] = (mix[0, rows, :] + ex_recv[1, rows, :].astype(F32)).astype(BF16)
        return carry

    lax.fori_loop(0, 8, block_out, 0)
    block_copy = pltpu.make_async_copy(out_ref, out_hbm, lsem.at[2, 0])
    block_copy.start()


    @pl.when(at.source)
    def _():
        far_copy().wait()
        near_copy(1 - at.hi).start()

    wait_all(kg_copies())
    for i in range(7):
        gker_ref[i] = finf[7 * i : 7 * i + 7, :] * scale

    for half in range(2):
        when(at.source, near_copy(half).wait_send)
        when(at.other, near_copy(half).wait_recv)
    for side, ref in ((0, ge_ref), (1, gc_ref)):
        for part in range(3):
            total = fin[0, side, part].astype(F32) + fin[1, side, part].astype(F32)
            ref[part * ROWS : (part + 1) * ROWS, :] = total * scale
    block_copy.wait()
    gimg_copy.wait()


def hand_over(*refs):
    n = len(refs) // 3
    sem = refs[-1]
    loads, stores = [], []
    for i in range(n):
        rows = refs[i].shape[0]
        step = 128 if rows == TOK else rows
        for k in range(0, rows, step):
            part = pl.ds(k, step)
            a, b, c = refs[i].at[part], refs[2 * n + i].at[part], refs[n + i].at[part]
            loads.append(pltpu.make_async_copy(a, b, sem.at[0, len(loads)]))
            stores.append(pltpu.make_async_copy(b, c, sem.at[1, len(stores)]))
    for cp in loads:
        cp.start()
    for load, store in zip(loads, stores):
        load.wait()
        store.start()
    for cp in stores:
        cp.wait()


def per_device(images, cotangent, dw_kernel, w_expand, w_contract):
    vmem = lambda: pl.BlockSpec(memory_space=pltpu.VMEM)
    anywhere = lambda: pl.BlockSpec(memory_space=pl.ANY)
    scratch = [
        pltpu.VMEM((TOK, C), BF16),
        pltpu.VMEM((TOK, C), BF16),
        pltpu.VMEM((TOK, C), BF16),
        pltpu.VMEM((2, 96, ROWS, C), BF16),
        pltpu.VMEM((2, 96, ROWS, C), BF16),
        pltpu.VMEM((2, TOK, C), BF16),
        pltpu.VMEM((2, TOK, C), BF16),
        pltpu.VMEM((2, TOK, C), F32),
        pltpu.VMEM((2, TOK, C), F32),
        pltpu.VMEM((2, TOK, C), BF16),
        pltpu.VMEM((2, TOK, C), BF16),
        pltpu.VMEM((TOK, C), F32),
        pltpu.VMEM((TOK, 128), F32),
        pltpu.VMEM((22, 32, 128), F32),
        pltpu.VMEM((49, 8, C), F32),
        pltpu.VMEM((64, C), F32),
                pltpu.VMEM((7, 8, C), F32),
        pltpu.VMEM((4, 8, C), F32),
        pltpu.VMEM((8, 8, C), F32),
        pltpu.VMEM((2, 2, 3, ROWS, C), BF16),
        pltpu.VMEM((64, C), F32),
        pltpu.VMEM((SPLIT, 2 * TOK, 3 * (32 // SPLIT) * ROWS), BF16),
    ]
    for part in range(3):
        for phase in range(3):
            scratch.append(pltpu.VMEM((3, 2, sizes(part)[phase], ROWS, C), BF16))
    for part in range(3):
        for phase in range(3):
            scratch.append(pltpu.VMEM((2, sizes(part)[phase], ROWS, C), BF16))
    scratch += [pltpu.SemaphoreType.DMA((3, 3, SPLIT, 4))] * 4
    scratch += [pltpu.SemaphoreType.DMA((4,))] * 2
    scratch += [pltpu.SemaphoreType.DMA((24,))] * 2
    scratch += [pltpu.SemaphoreType.DMA((3,))] * 2
    scratch += [pltpu.SemaphoreType.DMA((4, 4))]
    shapes = (
        jax.ShapeDtypeStruct((TOK, C), BF16),
        jax.ShapeDtypeStruct((TOK, C), BF16),
        jax.ShapeDtypeStruct((7, 7, C), F32),
        jax.ShapeDtypeStruct((48, C), F32),
        jax.ShapeDtypeStruct((48, C), F32),
    )
    results = pl.pallas_call(
        kernel,
        name="block_step",
        out_shape=shapes,
        in_specs=[anywhere(), anywhere(), vmem(), vmem(), vmem()],
        out_specs=(anywhere(), anywhere(), vmem(), vmem(), vmem()),
        scratch_shapes=scratch,
        compiler_params=pltpu.CompilerParams(
            collective_id=0, has_side_effects=True, vmem_limit_bytes=60 * 2**20
        ),
        cost_estimate=pl.CostEstimate(flops=15 * 10**9, bytes_accessed=10**7, transcendentals=10**6),
    )(
        images.reshape(TOK, C),
        cotangent.reshape(TOK, C),
        dw_kernel,
        w_expand,
        w_contract,
    )
    out, gimg, gker, ge, gc = pl.pallas_call(
        hand_over,
        name="hand_over",
        out_shape=shapes,
        in_specs=[anywhere() for _ in range(5)],
        out_specs=tuple(anywhere() for _ in range(5)),
        scratch_shapes=[pltpu.VMEM(a.shape, a.dtype) for a in shapes] + [pltpu.SemaphoreType.DMA((2, 11))],
    )(*results)
    return out.reshape(images.shape), gimg.reshape(images.shape), gker, ge, gc


def solution(mesh):
    tokens = P(("grp", "dev"), None, None, None)
    rows = P("dev", None)
    return jax.shard_map(
        per_device,
        mesh=mesh,
        in_specs=(tokens, tokens, P(), rows, rows),
        out_specs=(tokens, tokens, P(), rows, rows),
        check_vma=False,
    )
```

```python
import functools

import jax
import jax.numpy as jnp
from jax import lax
from jax.experimental import pallas as pl
from jax.experimental.pallas import tpu as pltpu
from jax.sharding import PartitionSpec as P

MESH = pl.DeviceIdType.MESH
F32, BF16 = jnp.float32, jnp.bfloat16
SQRT_HALF = 0.7071067811865476
INV_ROOT_TWO_PI = 0.3989422804014327
EPSILON = 1e-06
NT = (((1,), (1,)), ((), ()))
NN = (((1,), (0,)), ((), ()))
TN = (((0,), (0,)), ((), ()))

C = 768
TOK = 512
ROWS = 16
SPLIT = 4
ORDERS = (("x", "y", "z"), ("y", "z", "x"), ("z", "x", "y"))
SIZE = {"x": 2, "y": 4, "z": 4}


def dot(a, b, dims):
    return lax.dot_general(a, b, dims, preferred_element_type=F32)


def sizes(part):
    n = [SIZE[a] for a in ORDERS[part]]
    return (1, n[0], n[0] * n[1])


class Place:
    def __init__(self):
        grp, dev = lax.axis_index("grp"), lax.axis_index("dev")
        self.hi, self.core = grp // 2, grp % 2
        self.y, self.zlo, self.x = dev // 16, (dev // 4) % 4, dev % 4
        self.z = self.hi * 4 + self.zlo
        self.source = (self.x % 2) == self.core
        self.other = (self.x % 2) != self.core

    def device(self, x, y, z, core):
        return {"grp": (z // 4) * 2 + core, "dev": (y * 4 + z % 4) * 4 + x}

    def peer(self, axis, off, core=None):
        core = self.core if core is None else core
        x, y, z = self.x, self.y, self.z
        if axis == "x":
            x = (x + off + 4) % 4
        elif axis == "y":
            y = (y + off + 4) % 4
        else:
            z = (z + off + 8) % 8
        return self.device(x, y, z, core)

    def slot(self, axis, off=0):
        if axis == "x":
            return ((self.x + off + 4) % 4) // 2
        if axis == "y":
            return (self.y + off + 4) % 4
        return (self.zlo + off + 4) % 4

    def share(self, part, step):
        first = (self.y, self.zlo, 2 * (self.x // 2))[part]
        return (first + step) % SPLIT

    def runs(self, part, phase):
        order = ORDERS[part]
        n = [SIZE[a] for a in order]
        i = [self.slot(a) for a in order]
        share = n[0] * n[1] // SPLIT
        if phase == 1:
            first, count = i[1] * n[0], n[0]
        else:
            first, count = i[1] * n[0] + i[0], 1
        step = min(count, share)
        return [
            (where(part, (first + k) // share, i[2]) + (first + k) % share, step)
            for k in range(0, count, step)
        ]


def where(part, s, i3):
    share = sizes(part)[2] // SPLIT
    return s * (96 // SPLIT) + part * (32 // SPLIT) + i3 * share


def moves(axis):
    if axis == "z":
        return ((1, None, 0), (-1, None, 1), (2, 0, 2), (-2, 1, 3))
    return ((1, None, 0), (-1, None, 1), (2, None, 2))


def when(cond, fn):
    if cond is None:
        fn()
    else:
        pl.when(cond)(fn)


def kernel(
    img_hbm, cot_hbm, dwk_hbm, we_hbm, wc_hbm,
    out_hbm, gimg_hbm, gker_ref, ge_ref, gc_ref,
    img_ref, out_ref, gimg_ref, dwk_ref, we_ref, wc_ref, buf, grads, nrm2, cot2, mix, ngr, ex_send, ex_recv, conv, inv, pad, kacc,
    kall, krx, ky, kz, fin, finf, acts,
    rb0, rb1, rb2, rb3, rb4, rb5, rb6, rb7, rb8,
    t0, t1, t2, t3, t4, t5, t6, t7, t8,
    bsem_s, bsem_r, rsem_s, rsem_r, esem_s, esem_r, ksem_s, ksem_r, fsem_s, fsem_r, lsem,
):
    rbufs = ((rb0, rb1, rb2), (rb3, rb4, rb5), (rb6, rb7, rb8))
    tbufs = ((t0, t1, t2), (t3, t4, t5), (t6, t7, t8))
    at = Place()
    partner = at.device(at.x, at.y, at.z, 1 - at.core)

    barrier = pltpu.get_barrier_semaphore()
    friends = [at.peer("x", o) for o in (1, -1, 2)] + [at.peer("y", o) for o in (1, -1, 2)]
    friends += [at.peer("z", o) for o in range(1, 8)] + [partner]
    friends += [at.peer("x", o, 1 - at.core) for o in (1, -1, 2)]
    for friend in friends:
        pl.semaphore_signal(barrier, inc=1, device_id=friend, device_id_type=MESH)
    quarters = [pl.ds(i * 128, 128) for i in range(4)]
    img_in = [pltpu.make_async_copy(img_hbm.at[q], img_ref.at[q], lsem.at[0, i]) for i, q in enumerate(quarters)]
    cot_in = [pltpu.make_async_copy(cot_hbm.at[q], cot2.at[0, q], lsem.at[1, i]) for i, q in enumerate(quarters)]
    w_in = [pltpu.make_async_copy(we_hbm, we_ref, lsem.at[4, 0]), pltpu.make_async_copy(wc_hbm, wc_ref, lsem.at[4, 1])]
    dwk_in = pltpu.make_async_copy(dwk_hbm, dwk_ref, lsem.at[4, 2])
    for cp in w_in + img_in + [dwk_in] + cot_in:
        cp.start()
    pl.semaphore_wait(barrier, len(friends))

    def copy(src, dst, send, recv, to):
        return pltpu.make_async_remote_copy(
            src_ref=src, dst_ref=dst, send_sem=send, recv_sem=recv,
            device_id=to, device_id_type=MESH,
        )

    def gather_copies(part, phase, step=None, kind=None):
        axis = ORDERS[part][phase]
        px = ORDERS[part].index("x")
        if phase == 2:
            share, count = at.share(part, step), sizes(part)[2] // SPLIT
            runs = [(step, (where(part, share, at.slot(axis)), count))]
        else:
            runs = enumerate(at.runs(part, phase))
        if kind == "pass":
            out = []
            for off, half, j in ((1, 0, 2), (-1, 1, 3)):
                ref = buf.at[half, pl.ds(where(part, share, at.slot(axis, -off)), count)]
                cp = copy(ref, ref, bsem_s.at[part, phase, step, j], bsem_r.at[part, phase, step, j], at.peer(axis, off))
                out.append((cp, at.other if axis == "x" else None, at.source if axis == "x" else None))
            return out
        out = []
        for r, (start, count) in runs:
            for off, half, j in moves(axis)[: 2 if kind == "near" else 4]:
                if half is None:
                    ref = buf.at[:, pl.ds(start, count)]
                else:
                    ref = buf.at[half, pl.ds(start, count)]
                cp = copy(ref, ref, bsem_s.at[part, phase, r, j], bsem_r.at[part, phase, r, j], at.peer(axis, off))
                if phase < px:
                    send_if = recv_if = at.source
                elif phase == px:
                    send_if = at.source
                    recv_if = at.source if j == 2 else at.other
                else:
                    send_if = recv_if = None
                out.append((cp, send_if, recv_if))
        return out

    def gather_start(part, phase, step=None, kind=None):
        for cp, send_if, _ in gather_copies(part, phase, step, kind):
            when(send_if, cp.start)

    def gather_wait(part, phase, step=None, kind=None):
        for cp, send_if, recv_if in gather_copies(part, phase, step, kind):
            when(send_if, cp.wait_send)
            when(recv_if, cp.wait_recv)

    def gather_second():
        for part in range(3):
            gather_wait(part, 0)
        for part in range(3):
            gather_start(part, 1)
        gather_start(0, 2, 0)
        gather_start(1, 2, 0)

        @pl.when(at.source)
        def _():
            gather_start(2, 2, 0)
            gather_start(2, 2, 1, "near")

    def gather_third():
        for part in range(3):
            gather_wait(part, 1)

        @pl.when(at.other)
        def _():
            gather_start(2, 2, 0)

        gather_start(0, 2, 1, "near")
        gather_start(1, 2, 1, "near")

        @pl.when(at.other)
        def _():
            gather_start(2, 2, 1, "near")

        for step in range(2, SPLIT):
            for part in range(3):
                gather_start(part, 2, step, "near")

    def gather_pass(step):
        for part in range(3):
            gather_wait(part, 2, step, "near")
            gather_start(part, 2, step, "pass")

    for cp in w_in:
        cp.wait()

    @pl.when(at.source)
    def _():
        for part in range(3):
            ((start, _n),) = at.runs(part, 0)
            buf[0, start] = we_ref[part * ROWS : (part + 1) * ROWS]
            buf[1, start] = wc_ref[part * ROWS : (part + 1) * ROWS]

    for part in range(3):
        gather_start(part, 0)
    cot_copy = copy(cot_hbm, cot2.at[1], esem_s.at[0], esem_r.at[0], partner)
    cot_copy.start()

    pad[...] = jnp.zeros_like(pad)
    for cp in img_in + [dwk_in]:
        cp.wait()

    def windows(values):
        pad[3:19, 8:24, :] = values.reshape(16, 16, 128)

    def conv_step(i, source, target, flip, finish):
        image, block = i // 6, i % 6
        lanes = pl.ds(pl.multiple_of(block * 128, 128), 128)
        windows(source[pl.ds(pl.multiple_of(image * 256, 256), 256), lanes].astype(F32))
        for half in range(2):
            acc = jnp.zeros((8, 16, 128), F32)
            for q in range(7):
                shifted = pad[half * 8 : half * 8 + 14, 5 + q : 21 + q, :]
                for p in range(7):
                    tap = 48 - (p * 7 + q) if flip else p * 7 + q
                    acc = acc + shifted[p : p + 8] * dwk_ref[tap // 7, tap % 7 : tap % 7 + 1, lanes].reshape(1, 1, 128)
            rows = pl.ds(pl.multiple_of(image * 256 + half * 128, 128), 128)
            target[rows, lanes] = finish(acc.reshape(128, 128), rows, lanes)

    def forward(i, carry):
        conv_step(i, img_ref, conv, False, lambda v, rows, lanes: v)

        @pl.when(i == 6)
        def _():
            gather_second()

        return carry

    lax.fori_loop(0, 12, forward, 0)

    def norm(i, carry):
        rows = pl.ds(pl.multiple_of(i * 64, 64), 64)
        v = conv[rows, :]
        centred = v - jnp.mean(v, axis=1, keepdims=True)
        istd = lax.rsqrt(jnp.mean(centred * centred, axis=1, keepdims=True) + EPSILON)
        nrm2[0, rows, :] = (centred * istd).astype(BF16)
        inv[rows, :] = jnp.broadcast_to(istd, (64, 128))
        mix[0, rows, :] = img_ref[rows, :].astype(F32)
        mix[1, rows, :] = jnp.zeros((64, C), F32)
        ngr[0, rows, :] = jnp.zeros((64, C), F32)
        ngr[1, rows, :] = jnp.zeros((64, C), F32)
        return carry

    lax.fori_loop(0, 8, norm, 0)
    nrm_copy = copy(nrm2.at[0], nrm2.at[1], esem_s.at[1], esem_r.at[1], partner)
    nrm_copy.start()
    gather_third()
    for cp in cot_in:
        cp.wait()
    cot_copy.wait()
    nrm_copy.wait()

    def sides(part, phase):
        px = ORDERS[part].index("x")
        if phase < px:
            return (at.source,) * 4
        if phase == px:
            return at.other, at.source, at.source, at.source
        return (None,) * 4

    def reduce_last(part, step):
        axis = ORDERS[part][2]
        send_1, recv_1, send_2, recv_2 = sides(part, 2)
        share, count = at.share(part, step), sizes(part)[2] // SPLIT
        out = []
        for off, half, j in moves(axis):
            pieces = pl.ds(where(part, share, at.slot(axis, off)), count)
            lands = pl.ds(share * count, count)
            if half is None:
                a, b = grads.at[:, pieces], rbufs[part][2].at[j, :, lands]
            else:
                a, b = grads.at[half, pieces], rbufs[part][2].at[2, half, lands]
            cp = copy(a, b, rsem_s.at[part, 2, step, j], rsem_r.at[part, 2, step, j], at.peer(axis, off))
            out.append((cp, send_2 if j >= 2 else send_1, recv_2 if j >= 2 else recv_1))
        return out

    def reduce_middle(part, share, q):
        axis = ORDERS[part][1]
        send_1, recv_1, send_2, recv_2 = sides(part, 1)
        count = sizes(part)[2] // SPLIT
        per_block = sizes(part)[1] // count
        out = []
        for off, half, j in moves(axis):
            pieces, lands = pl.ds(share * count, count), pl.ds(q * count, count)
            src, dst = tbufs[part][2], rbufs[part][1]
            if half is None:
                a, b = src.at[:, pieces], dst.at[j, :, lands]
            else:
                a, b = src.at[half, pieces], dst.at[2, half, lands]
            cp = copy(a, b, rsem_s.at[part, 1, q, j], rsem_r.at[part, 1, q, j], at.peer(axis, off))
            goes = at.slot(axis, off) == share // per_block
            out.append((cp, goes, send_2 if j >= 2 else send_1, recv_2 if j >= 2 else recv_1))
        return out

    def reduce_first(part):
        axis = ORDERS[part][0]
        send_1, recv_1, send_2, recv_2 = sides(part, 0)
        out = []
        for off, half, j in moves(axis):
            pieces = pl.ds(at.slot(axis, off), 1)
            src, dst = tbufs[part][1], rbufs[part][0]
            if half is None:
                a, b = src.at[:, pieces], dst.at[j]
            else:
                a, b = src.at[half, pieces], dst.at[2, half]
            cp = copy(a, b, rsem_s.at[part, 0, 0, j], rsem_r.at[part, 0, 0, j], at.peer(axis, off))
            out.append((cp, send_2 if j >= 2 else send_1, recv_2 if j >= 2 else recv_1))
        return out

    def add_up(count, first, own, own_first, recv, dst):
        def piece(i, carry):
            for side in range(2):
                total = own[side, own_first + i].astype(F32) + recv[0, side, first + i].astype(F32)
                total = total + recv[1, side, first + i].astype(F32) + recv[2, side, first + i].astype(F32)
                dst[side, first + i] = total.astype(BF16)
            return carry

        lax.fori_loop(0, count, piece, 0)

    def reduce_start_last(step):
        for part in range(3):
            for cp, send_if, _ in reduce_last(part, step):
                when(send_if, cp.start)

    def reduce_second(step):
        for part in range(3):
            for cp, send_if, recv_if in reduce_last(part, step):
                when(send_if, cp.wait_send)
                when(recv_if, cp.wait_recv)
            share, count = at.share(part, step), sizes(part)[2] // SPLIT
            per_block = sizes(part)[1] // count

            def go(part=part, share=share, count=count, per_block=per_block):
                mine = where(part, share, at.slot(ORDERS[part][2]))
                add_up(count, share * count, grads, mine, rbufs[part][2], tbufs[part][2])
                for cp, goes, send_if, _ in reduce_middle(part, share, share % per_block):
                    when(goes if send_if is None else jnp.logical_and(goes, send_if), cp.start)

            when(at.source if ORDERS[part][2] == "x" else None, go)

    def reduce_third():
        for part in range(3):
            count = sizes(part)[2] // SPLIT
            per_block = sizes(part)[1] // count
            for q in range(per_block):
                for cp, _, send_if, recv_if in reduce_middle(part, q, q):
                    when(send_if, cp.wait_send)
                    when(recv_if, cp.wait_recv)

            def go(part=part):
                n1 = sizes(part)[1]
                add_up(n1, 0, tbufs[part][2], at.slot(ORDERS[part][1]) * n1, rbufs[part][1], tbufs[part][1])

            when(at.source if ORDERS[part].index("x") >= 1 else None, go)
            for cp, send_if, _ in reduce_first(part):
                when(send_if, cp.start)

    def reduce_end():
        for part in range(3):
            for cp, send_if, recv_if in reduce_first(part):
                when(send_if, cp.wait_send)
                when(recv_if, cp.wait_recv)

            def go(part=part):
                add_up(1, 0, tbufs[part][1], at.slot(ORDERS[part][0]), rbufs[part][0], tbufs[part][0])

            when(at.source, go)

    count = 32 // SPLIT
    width = 3 * count * ROWS

    def mix_step(step, carry):
        here = [pl.ds(where(part, at.share(part, step), 0), count) for part in range(3)]
        contract = jnp.concatenate([buf[1, h] for h in here]).reshape(width, C)
        mix[...] += dot(acts[step], contract, NN).reshape(2, TOK, C)
        return carry

    for part in range(3):
        gather_wait(part, 2, 0)

    def share_step(step, carry):
        @pl.when(step == 1)
        def _():
            gather_pass(2)

        @pl.when(step >= 1)
        def _():
            for part in range(3):
                gather_wait(part, 2, step, "pass")

        normed = nrm2[...].reshape(2 * TOK, C)
        upstream = cot2[...].reshape(2 * TOK, C)
        here = [pl.ds(where(part, at.share(part, step), 0), count) for part in range(3)]
        expand = jnp.concatenate([buf[0, h] for h in here]).reshape(width, C)
        contract = jnp.concatenate([buf[1, h] for h in here]).reshape(width, C)
        pre_act = dot(normed, expand, NT)
        act_grad = dot(upstream, contract, NT)
        cdf = 0.5 * (1.0 + lax.erf(pre_act * SQRT_HALF))
        activated = (pre_act * cdf).astype(BF16)
        slope = cdf + pre_act * jnp.exp(-0.5 * pre_act * pre_act) * INV_ROOT_TWO_PI
        pre_grad = (act_grad * slope).astype(BF16)
        grad_e = dot(pre_grad, normed, TN).astype(BF16).reshape(3, count, ROWS, C)
        grad_c = dot(activated, upstream, TN).astype(BF16).reshape(3, count, ROWS, C)
        for part in range(3):
            grads[0, here[part]] = grad_e[part]
            grads[1, here[part]] = grad_c[part]
        acts[step] = activated

        @pl.when(step <= 1)
        def _():
            gather_pass(2 * step + 1)

        reduce_start_last(step)
        ngr[...] += dot(pre_grad, expand, NN).reshape(2, TOK, C)

        @pl.when(step >= 2)
        def _():
            reduce_second(step - 2)

        return carry

    lax.fori_loop(0, SPLIT, share_step, 0)
    def send_back(i, source):
        def to_send(k, carry):
            rows = pl.ds(pl.multiple_of(k * 64, 64), 64)
            ex_send[i, rows, :] = source[1, rows, :].astype(BF16)
            return carry

        lax.fori_loop(0, 8, to_send, 0)
        cp = copy(ex_send.at[i], ex_recv.at[i], esem_s.at[2 + i], esem_r.at[2 + i], partner)
        cp.start()
        return cp

    ngr_copy = send_back(0, ngr)

    lax.fori_loop(0, 2, mix_step, 0)
    ngr_copy.wait()
    def norm_back(i, carry):
        rows = pl.ds(pl.multiple_of(i * 64, 64), 64)
        grad = ngr[0, rows, :] + ex_recv[0, rows, :].astype(F32)
        standard = nrm2[0, rows, :].astype(F32)
        mean = jnp.mean(grad, axis=1, keepdims=True)
        along = jnp.mean(grad * standard, axis=1, keepdims=True)
        conv[rows, :] = inv[rows, 0:1] * (grad - mean - standard * along)
        return carry

    lax.fori_loop(0, 8, norm_back, 0)

    def kernel_terms(block, carry):
        @pl.when(jnp.logical_or(block == 0, block == 4))
        def _():
            reduce_second(2 + block // 4)

        lanes = pl.ds(pl.multiple_of(block * 128, 128), 128)
        for image in range(2):
            windows(img_ref[image * 256 : image * 256 + 256, lanes].astype(F32))
            for half in range(2):
                first = image * 256 + half * 128
                g = conv[first : first + 128, lanes].reshape(8, 16, 128)
                for q in range(7):
                    shifted = pad[half * 8 : half * 8 + 14, 5 + q : 21 + q, :]
                    for p in range(7):
                        r = jnp.sum((g * shifted[p : p + 8]).reshape(16, 8, 128), axis=0)
                        if image == 0 and half == 0:
                            kacc[p * 7 + q, :, lanes] = r
                        else:
                            kacc[p * 7 + q, :, lanes] += r
        return carry

    lax.fori_loop(0, 6, kernel_terms, 0)
    kall[49:64, :] = jnp.zeros((15, C), F32)
    kall[0:49, :] = jnp.sum(kacc[...], axis=1)

    plane = [(0, 1 - at.core)] + [(off, core) for off in (1, -1, 2) for core in (at.core, 1 - at.core)]

    def kx_copies():
        out = []
        for j, (off, core) in enumerate(plane):
            rows = pl.ds(core * 32 + ((at.x + off + 4) % 4) * 8, 8)
            out.append(copy(kall.at[rows], krx.at[j], ksem_s.at[j], ksem_r.at[j], at.peer("x", off, core)))
        return out

    def ky_copies():
        return [
            copy(ky.at[at.y], ky.at[at.y], ksem_s.at[7 + j], ksem_r.at[7 + j], at.peer("y", off))
            for j, off in enumerate((1, -1, 2))
        ]

    def kz_copies():
        return [
            copy(kz.at[at.z], kz.at[at.z], ksem_s.at[10 + j], ksem_r.at[10 + j], at.peer("z", off))
            for j, off in enumerate((4, 3, 5, 2, 6, 1, 7))
        ]

    share = pl.ds(at.core * 32 + at.x * 8, 8)

    def kg_copies():
        return [
            copy(finf.at[share], finf.at[share], ksem_s.at[17 + j], ksem_r.at[17 + j], at.peer("x", off, core))
            for j, (off, core) in enumerate(plane)
        ]

    def start_all(copies):
        for cp in copies:
            cp.start()

    def wait_all(copies):
        for cp in copies:
            cp.wait()

    start_all(kx_copies())

    scale = float(TOK * 256) ** (-0.5)

    far = at.peer("z", 4)

    def far_copy():
        return copy(fin.at[at.hi], fin.at[at.hi], fsem_s.at[0], fsem_r.at[0], far)

    def near_copy(half):
        return copy(fin.at[half], fin.at[half], fsem_s.at[half + 1], fsem_r.at[half + 1], partner)

    def far_start():
        @pl.when(at.source)
        def _():
            for part in range(3):
                for side in range(2):
                    fin[at.hi, side, part] = tbufs[part][0][side, 0]
            far_copy().start()
            near_copy(at.hi).start()

    def backward(i, carry):
        conv_step(
            i, conv, gimg_ref, True,
            lambda v, rows, lanes: (v + cot2[0, rows, lanes].astype(F32)).astype(BF16),
        )

        @pl.when(i == 5)
        def _():
            reduce_third()

        @pl.when(i == 6)
        def _():
            wait_all(kx_copies())
            total = kall[pl.ds(pl.multiple_of(at.core * 32 + at.x * 8, 8), 8), :]
            for j in range(7):
                total = total + krx[j]
            ky[at.y] = total
            start_all(ky_copies())

        return carry

    lax.fori_loop(0, 12, backward, 0)
    gimg_copy = pltpu.make_async_copy(gimg_ref, gimg_hbm, lsem.at[3, 0])
    gimg_copy.start()
    wait_all(ky_copies())
    kz[at.z] = ky[0] + ky[1] + ky[2] + ky[3]
    start_all(kz_copies())
    reduce_end()
    far_start()
    mix_step(2, 0)
    mix_step(3, 0)
    mix_copy = send_back(1, mix)
    wait_all(kz_copies())
    total = kz[0]
    for i in range(1, 8):
        total = total + kz[i]
    finf[pl.ds(pl.multiple_of(at.core * 32 + at.x * 8, 8), 8), :] = total
    start_all(kg_copies())
    mix_copy.wait()

    def block_out(i, carry):
        rows = pl.ds(pl.multiple_of(i * 64, 64), 64)
        out_ref[rows, :] = (mix[0, rows, :] + ex_recv[1, rows, :].astype(F32)).astype(BF16)
        return carry

    lax.fori_loop(0, 8, block_out, 0)
    block_copy = pltpu.make_async_copy(out_ref, out_hbm, lsem.at[2, 0])
    block_copy.start()


    @pl.when(at.source)
    def _():
        far_copy().wait()
        near_copy(1 - at.hi).start()

    wait_all(kg_copies())
    for i in range(7):
        gker_ref[i] = finf[7 * i : 7 * i + 7, :] * scale

    for half in range(2):
        when(at.source, near_copy(half).wait_send)
        when(at.other, near_copy(half).wait_recv)
    for side, ref in ((0, ge_ref), (1, gc_ref)):
        for part in range(3):
            total = fin[0, side, part].astype(F32) + fin[1, side, part].astype(F32)
            ref[part * ROWS : (part + 1) * ROWS, :] = total * scale
    block_copy.wait()
    gimg_copy.wait()


def hand_over(*refs):
    n = len(refs) // 3
    sem = refs[-1]
    loads, stores = [], []
    for i in range(n):
        rows = refs[i].shape[0]
        step = 128 if rows == TOK else rows
        for k in range(0, rows, step):
            part = pl.ds(k, step)
            a, b, c = refs[i].at[part], refs[2 * n + i].at[part], refs[n + i].at[part]
            loads.append(pltpu.make_async_copy(a, b, sem.at[0, len(loads)]))
            stores.append(pltpu.make_async_copy(b, c, sem.at[1, len(stores)]))
    for cp in loads:
        cp.start()
    for load, store in zip(loads, stores):
        load.wait()
        store.start()
    for cp in stores:
        cp.wait()


def per_device(images, cotangent, dw_kernel, w_expand, w_contract):
    vmem = lambda: pl.BlockSpec(memory_space=pltpu.VMEM)
    anywhere = lambda: pl.BlockSpec(memory_space=pl.ANY)
    scratch = [
        pltpu.VMEM((TOK, C), BF16),
        pltpu.VMEM((TOK, C), BF16),
        pltpu.VMEM((TOK, C), BF16),
        pltpu.VMEM((7, 7, C), F32),
        pltpu.VMEM((48, C), BF16),
        pltpu.VMEM((48, C), BF16),
        pltpu.VMEM((2, 96, ROWS, C), BF16),
        pltpu.VMEM((2, 96, ROWS, C), BF16),
        pltpu.VMEM((2, TOK, C), BF16),
        pltpu.VMEM((2, TOK, C), BF16),
        pltpu.VMEM((2, TOK, C), F32),
        pltpu.VMEM((2, TOK, C), F32),
        pltpu.VMEM((2, TOK, C), BF16),
        pltpu.VMEM((2, TOK, C), BF16),
        pltpu.VMEM((TOK, C), F32),
        pltpu.VMEM((TOK, 128), F32),
        pltpu.VMEM((22, 32, 128), F32),
        pltpu.VMEM((49, 8, C), F32),
        pltpu.VMEM((64, C), F32),
                pltpu.VMEM((7, 8, C), F32),
        pltpu.VMEM((4, 8, C), F32),
        pltpu.VMEM((8, 8, C), F32),
        pltpu.VMEM((2, 2, 3, ROWS, C), BF16),
        pltpu.VMEM((64, C), F32),
        pltpu.VMEM((SPLIT, 2 * TOK, 3 * (32 // SPLIT) * ROWS), BF16),
    ]
    for part in range(3):
        for phase in range(3):
            scratch.append(pltpu.VMEM((3, 2, sizes(part)[phase], ROWS, C), BF16))
    for part in range(3):
        for phase in range(3):
            scratch.append(pltpu.VMEM((2, sizes(part)[phase], ROWS, C), BF16))
    scratch += [pltpu.SemaphoreType.DMA((3, 3, SPLIT, 4))] * 4
    scratch += [pltpu.SemaphoreType.DMA((4,))] * 2
    scratch += [pltpu.SemaphoreType.DMA((24,))] * 2
    scratch += [pltpu.SemaphoreType.DMA((3,))] * 2
    scratch += [pltpu.SemaphoreType.DMA((5, 4))]
    shapes = (
        jax.ShapeDtypeStruct((TOK, C), BF16),
        jax.ShapeDtypeStruct((TOK, C), BF16),
        jax.ShapeDtypeStruct((7, 7, C), F32),
        jax.ShapeDtypeStruct((48, C), F32),
        jax.ShapeDtypeStruct((48, C), F32),
    )
    results = pl.pallas_call(
        kernel,
        name="block_step",
        out_shape=shapes,
        in_specs=[anywhere() for _ in range(5)],
        out_specs=(anywhere(), anywhere(), vmem(), vmem(), vmem()),
        scratch_shapes=scratch,
        compiler_params=pltpu.CompilerParams(
            collective_id=0, has_side_effects=True, vmem_limit_bytes=60 * 2**20
        ),
        cost_estimate=pl.CostEstimate(flops=15 * 10**9, bytes_accessed=10**7, transcendentals=10**6),
    )(
        images.reshape(TOK, C),
        cotangent.reshape(TOK, C),
        dw_kernel,
        w_expand,
        w_contract,
    )
    out, gimg, gker, ge, gc = pl.pallas_call(
        hand_over,
        name="hand_over",
        out_shape=shapes,
        in_specs=[anywhere() for _ in range(5)],
        out_specs=tuple(anywhere() for _ in range(5)),
        scratch_shapes=[pltpu.VMEM(a.shape, a.dtype) for a in shapes] + [pltpu.SemaphoreType.DMA((2, 11))],
    )(*results)
    return out.reshape(images.shape), gimg.reshape(images.shape), gker, ge, gc


def solution(mesh):
    tokens = P(("grp", "dev"), None, None, None)
    rows = P("dev", None)
    return jax.shard_map(
        per_device,
        mesh=mesh,
        in_specs=(tokens, tokens, P(), rows, rows),
        out_specs=(tokens, tokens, P(), rows, rows),
        check_vma=False,
    )
```
